128 devices in a mesh: rows: 64 (over x, z, y), blk: 2 (over core).
Axes of the slice: x: 4, y: 4, z: 4, core: 2. Of those that a mesh axis runs over, the one named last changes fastest.
Arguments:
- off_blocks: bfloat16 [2048, 6, 192, 192], P('rows', None, 'blk'), may hold values from -0.15625 to 0.15625
- diag_blocks: bfloat16 [2048, 192, 192], P('rows', 'blk')
- precond: bfloat16 [2048, 192, 192], P('rows', 'blk')
- adj_rhs: float32 [2048, 16, 192], P('rows'), may hold values from -6 to 6
- col_owner: int32 [2048, 6], P('rows'), may hold values from 0 to 63, as said below
- col_local: int32 [2048, 6], P('rows'), may hold values from 0 to 31
Outputs:
- adjoint: float32 [2048, 16, 192], P('rows')
- residual: float32 [2048, 16, 192], P('rows')
The draws below stay inside these ranges and needn't reach their ends.
Inputs may be any that keep to these rules, and one draw needn't show every extreme that they name: `col_owner`: for a block row held by device r, entry k is r itself or (r + o) mod 64, where o is the k-th of 1, 63, 2, 62, 32, 33. In one device's block rows, at most 16 entries of one column differ from the device's own index, at least one does, and on every device some column has exactly 16 such entries.
All inputs are finite; a program needn't handle non-finite values.
Results may differ from the reference program's by a relative error of at most 0.011.
Values may be sent and summed in bfloat16 or wider, within the bound.
No kernel may reach another device: no remote copies, remote signals or barrier semaphores. Data moves between devices by JAX's collectives and lax.ppermute only.
A program may use at most 128 MiB of HBM per device.

```python
import jax
import jax.numpy as jnp
from jax import lax

B = 192
NADJ = 16
ITERS = 2
BR_DEV = 32
NB = 2048
CAP = 16
N_ROWS = 64


def draw_diag_blocks(key, part):
    key = jax.random.fold_in(key, 3)
    noise = jax.random.normal(key, (NB, B, B), jnp.float32) * 0.1
    return (4.0 * jnp.eye(B, dtype=jnp.float32)[None] + noise).astype(jnp.bfloat16)


def draw_precond(key, part):
    key = jax.random.fold_in(key, 5)
    noise = jax.random.normal(key, (NB, B, B), jnp.float32) * 0.02
    return (0.25 * jnp.eye(B, dtype=jnp.float32)[None] + noise).astype(jnp.bfloat16)


def draw_col_owner(key, part):
    half_way = N_ROWS // 2
    offsets = jnp.array([1, N_ROWS - 1, 2, N_ROWS - 2, half_way, half_way + 1], dtype=jnp.int32)
    base = jax.random.fold_in(key, 17)
    key_count, key_face, key_perm = jax.random.split(base, 3)
    counts = jax.random.randint(key_count, (N_ROWS, 6), 1, CAP + 1)
    full_face = jax.random.randint(key_face, (N_ROWS,), 0, 6)
    faces = jnp.arange(6, dtype=jnp.int32)
    counts = jnp.where(faces[None, :] == full_face[:, None], CAP, counts).astype(jnp.int32)
    perm_keys = jax.random.split(key_perm, N_ROWS * 6)
    orders = jax.vmap(lambda one_key: jax.random.permutation(one_key, BR_DEV))(perm_keys)
    position = jnp.argsort(orders.reshape(N_ROWS, 6, BR_DEV), axis=-1).astype(jnp.int32)
    remote = position < counts[:, :, None]
    device = jnp.arange(N_ROWS, dtype=jnp.int32)[:, None, None]
    neighbour = (device + offsets[None, :, None]) % N_ROWS
    owner = jnp.where(remote, neighbour, device)
    return jnp.transpose(owner, (0, 2, 1)).reshape(NB, 6).astype(jnp.int32)


def plant(values, key, least, high):
    extent = values.shape
    spot = [jax.random.randint(jax.random.fold_in(key, axis), (), 0, extent[axis]) for axis in range(len(extent))]
    values = values.at[tuple(spot)].set(least)
    longest = extent.index(max(extent))
    spot[longest] = (spot[longest] + 1) % extent[longest]
    return values.at[tuple(spot)].set(high)


def block_scale(stream_key, shape, pieces, smallest, high):
    factor_of, own = 1.0, jax.random.fold_in(stream_key, 6)
    for axis_at, parts in pieces:
        steps = jnp.exp(jax.random.uniform(jax.random.fold_in(own, axis_at), (parts,), jnp.float32, smallest / len(pieces), high / len(pieces)))
        factor_of = factor_of * jnp.repeat(steps, shape[axis_at] // parts).reshape([-1 if axis == axis_at else 1 for axis in range(len(shape))])
    return factor_of


def normal_values(stream_key, shape, deviation, limit, cuts=(), kind=jnp.bfloat16):
    values = deviation * jax.random.normal(stream_key, shape, jnp.float32)
    if cuts:
        values = values * block_scale(stream_key, shape, cuts, -0.22, 0.18)
    return jnp.clip(values, -limit, limit).astype(kind)


def setup_inputs(seed: int = 0) -> dict:
    splits = jax.random.split(jax.random.key(seed), 7)
    off_blocks = normal_values(splits[0], (NB, 6, B, B), (8 * B) ** -0.5, 0.15625, ((0, 64), (2, 2)))
    diag_blocks = draw_diag_blocks(jax.random.fold_in(splits[6], 71), 0)
    precond = draw_precond(jax.random.fold_in(splits[6], 71), 0)
    adj_rhs = normal_values(splits[3], (NB, NADJ, B), 1.0, 6.0, ((0, 64),), jnp.float32)
    col_owner = draw_col_owner(jax.random.fold_in(splits[6], 71), 0)
    col_local = plant(jax.random.randint(splits[5], (NB, 6), 0, BR_DEV), jax.random.fold_in(splits[5], 1), 0, BR_DEV - 1).astype(jnp.int32)
    return {"off_blocks": off_blocks, "diag_blocks": diag_blocks, "precond": precond, "adj_rhs": adj_rhs, "col_owner": col_owner, "col_local": col_local}


def precondition(precond_full, field):
    rounded = lax.optimization_barrier(field.astype(jnp.bfloat16)).astype(jnp.float32)
    return jnp.einsum('nrc,nac->nar', precond_full, rounded, precision=lax.Precision.HIGHEST)


def transposed(off_blocks, diag_full, cols, xb):
    field = xb.astype(jnp.float32)
    result = jnp.einsum('nrc,nar->nac', diag_full, field, precision=lax.Precision.HIGHEST)
    for k in range(6):
        block = off_blocks[:, k].astype(jnp.float32)
        term = jnp.einsum('nrc,nar->nac', block, field, precision=lax.Precision.HIGHEST)
        result = result.at[cols[:, k]].add(term)
    return result


def reference(off_blocks, diag_blocks, precond, adj_rhs, col_owner, col_local):
    cols = (col_owner * BR_DEV + col_local).astype(jnp.int32)
    precond_full = precond.astype(jnp.float32)
    diag_full = diag_blocks.astype(jnp.float32)
    adjoint = precondition(precond_full, adj_rhs)
    residual = adj_rhs
    for step in range(ITERS):
        xb = adjoint.astype(jnp.bfloat16)
        residual = adj_rhs - transposed(off_blocks, diag_full, cols, xb)
        adjoint = adjoint + precondition(precond_full, residual)
    return adjoint, residual
```

```python
import functools

import jax
import jax.numpy as jnp
from jax import lax
from jax.experimental import pallas as pl
from jax.experimental.pallas import tpu as pltpu
from jax.sharding import PartitionSpec as P

ROWS = 32
FAN = 6
ADJ = 16
WIDTH = 192
HALF = 96
CAP = 16
BODY = CAP * ADJ * WIDTH // 128
WIDE = CAP * ADJ
FACES = ((0, 2), (1, 3), (4, 5))
SLOTS = ROWS + FAN * CAP
CHUNKS = 8
PER = ROWS // CHUNKS
VMEM_LIMIT = 48 * 1024 * 1024

VM = pl.BlockSpec(memory_space=pltpu.VMEM)
SM = pl.BlockSpec(memory_space=pltpu.SMEM)
ANY = pl.BlockSpec(memory_space=pl.ANY)


def my_face(p, core):
    return jnp.where(core == 0, FACES[p][0], FACES[p][1])


def load_blocks(hbm, vmem, sems):
    copies = []
    for chunk in range(CHUNKS):
        part = pl.ds(chunk * PER, PER)
        copies.append([pltpu.make_async_copy(h.at[part], v.at[part], sems.at[k, chunk]) for k, (h, v) in enumerate(zip(hbm, vmem))])
    return copies


def terms_phase(copies, x_half, off_v, diag_v, owner, local, sums, labels):
    own = lax.axis_index("rows")
    sums[...] = jnp.zeros(sums.shape, sums.dtype)
    if labels is not None:
        labels[...] = jnp.zeros(labels.shape, labels.dtype)

    def row(i, ranks):
        x = x_half[i].astype(jnp.bfloat16)
        terms = [jnp.dot(x, diag_v[i], preferred_element_type=jnp.float32)]
        places, after = [i], []
        for k in range(FAN):
            terms.append(jnp.dot(x, off_v[i, k], preferred_element_type=jnp.float32))
            remote = owner[k, i] != own
            places.append(jnp.where(remote, ROWS + k * CAP + ranks[k], local[k, i]))
            after.append(ranks[k] + remote.astype(jnp.int32))
        for place, term in zip(places, terms):
            sums[place] = sums[place] + term
        if labels is not None:
            for k in range(FAN):
                labels[pl.ds(places[k + 1], 1), :] = jnp.full((1, 128), local[k, i] + 1, jnp.int32).astype(jnp.float32)
        return tuple(after)

    ranks = (jnp.int32(0),) * FAN
    for chunk in range(CHUNKS):
        for copy in copies[chunk]:
            copy.wait()
        ranks = lax.fori_loop(chunk * PER, (chunk + 1) * PER, row, ranks, unroll=True)


def pack(sums, face):
    slots = pl.ds(ROWS + face * CAP, CAP)
    wide = sums[slots, :, 0:128].reshape(WIDE, 128)
    low = sums[pl.ds(ROWS + face * CAP, CAP // 2), :, 128:WIDTH]
    high = sums[pl.ds(ROWS + face * CAP + CAP // 2, CAP // 2), :, 128:WIDTH]
    narrow = jnp.concatenate([low, high], axis=2).reshape(WIDE // 2, 128)
    return wide, narrow


def emit(sums, labels, mine, theirs, partial):
    core = lax.axis_index("blk")
    partial[...] = sums[0:ROWS]
    for p in range(len(FACES)):
        face = my_face(p, core)
        wide, narrow = pack(sums, face)
        mine[p][0:WIDE] = wide
        mine[p][WIDE:BODY] = narrow
        if labels is not None:
            mine[p][BODY:] = labels[pl.ds(ROWS + face * CAP, CAP), :]
        wide, narrow = pack(sums, my_face(p, 1 - core))
        theirs[p][0:WIDE] = wide.astype(jnp.bfloat16)
        theirs[p][WIDE:BODY] = narrow.astype(jnp.bfloat16)
        if labels is not None:
            theirs[p][BODY:] = jnp.zeros((CAP, 128), jnp.bfloat16)


def solve(field, block):
    return lax.dot_general(field.astype(jnp.bfloat16), block, (((1,), (1,)), ((), ())), preferred_element_type=jnp.float32)


def first_kernel(off, diag, precond, rhs, owner, local, x_half, partial, m0, m1, m2, t0, t1, t2, off_v, diag_v, pre_v, sums, labels, sems, pre_sem):
    pre_copy = pltpu.make_async_copy(precond, pre_v, pre_sem)
    pre_copy.start()
    copies = load_blocks((off, diag), (off_v, diag_v), sems)
    for chunk in copies:
        for copy in chunk:
            copy.start()
    pre_copy.wait()

    def row(n, _):
        x_half[n] = solve(rhs[n], pre_v[n])
        return 0

    lax.fori_loop(0, ROWS, row, 0, unroll=4)
    terms_phase(copies, x_half, off_v, diag_v, owner, local, sums, labels)
    emit(sums, labels, (m0, m1, m2), (t0, t1, t2), partial)


def place(messages, label_of, first, narrow_sum, wide_sum):
    wide_sum[...] = jnp.zeros(wide_sum.shape, wide_sum.dtype)
    narrow_sum[...] = jnp.zeros(narrow_sum.shape, narrow_sum.dtype)
    lane = lax.broadcasted_iota(jnp.int32, (ADJ, 128), 1)
    for p, message in enumerate(messages):
        for s in range(CAP // 2):
            at = []
            for slot in (s, s + CAP // 2):
                label = label_of(first + p * CAP + slot)
                at.append(jnp.where(label == 0, ROWS, label - 1))
                wide_sum[at[-1]] += message[slot * ADJ : (slot + 1) * ADJ].astype(jnp.float32)
            both = message[WIDE + s * ADJ : WIDE + (s + 1) * ADJ].astype(jnp.float32)
            narrow_sum[at[0]] += jnp.where(lane < 64, both, 0.0)
            narrow_sum[at[1]] += jnp.where(lane < 64, 0.0, both)


def read_labels(messages, row_v, labels_s, sem):
    found = jnp.concatenate([m[BODY:].astype(jnp.float32) for m in messages], axis=0)
    rows = lax.broadcasted_iota(jnp.int32, found.shape, 0)
    lanes = lax.broadcasted_iota(jnp.int32, found.shape, 1)
    row = jnp.sum(jnp.where(rows == lanes, found, 0.0), axis=0, keepdims=True)
    row_v[...] = row.astype(jnp.int32)
    copy = pltpu.make_async_copy(row_v, labels_s, sem)
    copy.start()
    return copy


def residual_of(n, rhs, ours, other, wides, narrows):
    narrow = narrows[0][n] + narrows[1][n]
    narrow = narrow + pltpu.roll(narrow, 64, 1)
    got = jnp.concatenate([wides[0][n] + wides[1][n], narrow[:, 0:64]], axis=1)
    return rhs[n] - ((ours[n] + other[n]) + got)


def middle_kernel(off, diag, precond, rhs, owner, local, x_before, ours, other, g0, g1, g2, f0, f1, f2,
                  residual, labels_out, partial, m0, m1, m2, t0, t1, t2,
                  off_v, diag_v, pre_v, sums, x_half, wide_a, wide_b, narrow_a, narrow_b, row_v, sems, pre_sem, label_sem):
    pre_copy = pltpu.make_async_copy(precond, pre_v, pre_sem)
    pre_copy.start()
    copies = load_blocks((off, diag), (off_v, diag_v), sems)
    for chunk in copies:
        for copy in chunk:
            copy.start()
    label_copy = read_labels((g0, g1, g2, f0, f1, f2), row_v, labels_out, label_sem)
    label_copy.wait()
    label_of = lambda at: labels_out[0, at]
    place((g0, g1, g2), label_of, 0, narrow_a, wide_a)
    place((f0, f1, f2), label_of, 3 * CAP, narrow_b, wide_b)
    pre_copy.wait()

    def row(n, _):
        left = residual_of(n, rhs, ours, other, (wide_a, wide_b), (narrow_a, narrow_b))
        residual[n] = left
        x_half[n] = x_before[n] + solve(left, pre_v[n])
        return 0

    lax.fori_loop(0, ROWS, row, 0, unroll=4)
    terms_phase(copies, x_half, off_v, diag_v, owner, local, sums, None)
    emit(sums, None, (m0, m1, m2), (t0, t1, t2), partial)


def last_kernel(precond, precond_other, rhs, before, ours, other, labels, g0, g1, g2, f0, f1, f2,
                adjoint, residual, pre_v, wide_a, wide_b, narrow_a, narrow_b, pre_sem):
    core = lax.axis_index("blk")
    mine = pltpu.make_async_copy(precond, pre_v.at[core], pre_sem.at[0])
    theirs = pltpu.make_async_copy(precond_other, pre_v.at[1 - core], pre_sem.at[1])
    mine.start()
    theirs.start()
    label_of = lambda at: labels[0, at]
    place((g0, g1, g2), label_of, 0, narrow_a, wide_a)
    place((f0, f1, f2), label_of, 3 * CAP, narrow_b, wide_b)
    mine.wait()
    theirs.wait()

    def row(n, _):
        left = residual_of(n, rhs, ours, other, (wide_a, wide_b), (narrow_a, narrow_b))
        residual[n] = left
        fields = jnp.concatenate([left, before[n], rhs[n]], axis=0)
        for half in range(2):
            three = solve(fields, pre_v[half, n])
            adjoint[n, :, half * HALF : (half + 1) * HALF] = (three[2 * ADJ :] + three[ADJ : 2 * ADJ]) + three[0:ADJ]
        return 0

    lax.fori_loop(0, ROWS, row, 0, unroll=4)


def params():
    return pltpu.CompilerParams(vmem_limit_bytes=VMEM_LIMIT)


def on_device(off_blocks, diag_blocks, precond, adj_rhs, col_owner, col_local):
    nrows = lax.axis_size("rows")
    offsets = (1, nrows - 1, 2, nrows - 2, nrows // 2, nrows // 2 + 1)
    shape = jax.ShapeDtypeStruct
    field = shape((ROWS, ADJ, WIDTH), jnp.float32)
    half_field = shape((ROWS, ADJ, HALF), jnp.float32)

    def across(x):
        return lax.ppermute(x, "blk", [(0, 1), (1, 0)])

    def to_faces(x, p):
        pairs = [(2 * i + c, 2 * ((i + offsets[FACES[p][c]]) % nrows) + c) for i in range(nrows) for c in range(2)]
        return lax.ppermute(x, ("rows", "blk"), pairs)

    def exchange(partial, mine, theirs):
        got = []
        for p in range(len(FACES)):
            sending = (mine[p] + across(theirs[p]).astype(jnp.float32)).astype(jnp.bfloat16)
            got.append(to_faces(sending, p))
        other = across(partial)
        forwarded = [across(g) for g in got]
        return other, got, forwarded

    blocks = [
        pltpu.VMEM((ROWS, FAN, HALF, WIDTH), jnp.bfloat16),
        pltpu.VMEM((ROWS, HALF, WIDTH), jnp.bfloat16),
        pltpu.VMEM((ROWS, HALF, WIDTH), jnp.bfloat16),
        pltpu.VMEM((SLOTS, ADJ, WIDTH), jnp.float32),
    ]
    sums_of_messages = [pltpu.VMEM((ROWS + 1, ADJ, 128), jnp.float32)] * 4
    owner, local = col_owner.T, col_local.T
    precond_other = across(precond)

    x_half, partial, *messages = pl.pallas_call(
        first_kernel,
        out_shape=[half_field, field] + [shape((BODY + CAP, 128), jnp.float32)] * 3 + [shape((BODY + CAP, 128), jnp.bfloat16)] * 3,
        in_specs=[ANY, ANY, ANY, VM, SM, SM],
        out_specs=[VM] * 8,
        scratch_shapes=blocks + [pltpu.VMEM((SLOTS, 128), jnp.float32), pltpu.SemaphoreType.DMA((2, CHUNKS)), pltpu.SemaphoreType.DMA],
        compiler_params=params(),
        name="first_terms",
    )(off_blocks, diag_blocks, precond, adj_rhs, owner, local)
    other, got, forwarded = exchange(partial, messages[:3], messages[3:])

    before, labels, partial, *messages = pl.pallas_call(
        middle_kernel,
        out_shape=[field, shape((1, 128), jnp.int32), field] + [shape((BODY, 128), jnp.float32)] * 3 + [shape((BODY, 128), jnp.bfloat16)] * 3,
        in_specs=[ANY, ANY, ANY, VM, SM, SM] + [VM] * 9,
        out_specs=[VM, SM] + [VM] * 7,
        scratch_shapes=blocks + [pltpu.VMEM((ROWS, ADJ, HALF), jnp.float32)] + sums_of_messages
        + [pltpu.VMEM((1, 128), jnp.int32), pltpu.SemaphoreType.DMA((2, CHUNKS)), pltpu.SemaphoreType.DMA, pltpu.SemaphoreType.DMA],
        compiler_params=params(),
        name="residual_and_terms",
    )(off_blocks, diag_blocks, precond, adj_rhs, owner, local, x_half, partial, other, *got, *forwarded)
    other, got, forwarded = exchange(partial, messages[:3], messages[3:])

    return pl.pallas_call(
        last_kernel,
        out_shape=[field, field],
        in_specs=[ANY, ANY] + [VM] * 4 + [SM] + [VM] * 6,
        out_specs=[VM] * 2,
        scratch_shapes=[pltpu.VMEM((2, ROWS, HALF, WIDTH), jnp.bfloat16)] + sums_of_messages + [pltpu.SemaphoreType.DMA((2,))],
        compiler_params=params(),
        name="last_residual",
    )(precond, precond_other, adj_rhs, before, partial, other, labels, *got, *forwarded)


def solution(mesh):
    in_specs = (
        P("rows", None, "blk", None),
        P("rows", "blk", None),
        P("rows", "blk", None),
        P("rows", None, None),
        P("rows", None),
        P("rows", None),
    )
    out_specs = (P("rows", None, None), P("rows", None, None))

    def program(*arrays):
        return tuple(on_device(*arrays))

    return jax.shard_map(program, mesh=mesh, in_specs=in_specs, out_specs=out_specs, check_vma=False)
```

```python
import jax
import jax.numpy as jnp
from jax import lax
from jax.experimental import pallas as pl
from jax.experimental.pallas import tpu as pltpu
from jax.sharding import PartitionSpec as P

ROWS = 32
FAN = 6
ADJ = 16
WIDTH = 192
HALF = 96
CAP = 16
WIDE = CAP * ADJ
BODY = WIDE + WIDE // 2
NEAR, SEAM, FAR = 0, 1, 2
ORDER = (FAR, SEAM, NEAR)
FACES = (
    ((0, 1, 0, 1), (2, 2, 3, 3)),
    ((1, 0, 1, 0), (3, 3, 2, 2)),
    ((4, 4, 4, 4), (5, 5, 5, 5)),
)
STRIDE = CAP + 1
COUNTS = FAN * STRIDE
CHUNKS = 8
PIECES = 4
PIECE = ROWS // PIECES
PER = ROWS // CHUNKS
VMEM_LIMIT = 24 * 1024 * 1024

VM = pl.BlockSpec(memory_space=pltpu.VMEM)
SM = pl.BlockSpec(memory_space=pltpu.SMEM)
ANY = pl.BlockSpec(memory_space=pl.ANY)
HBM = pl.BlockSpec(memory_space=pltpu.HBM)


def face_of(p, core, own):
    kind = lax.rem(own, 4)
    picks = []
    for faces in FACES[ORDER[p]]:
        pick = faces[3]
        for k in (2, 1, 0):
            pick = jnp.where(kind == k, faces[k], pick)
        picks.append(pick)
    return jnp.where(core == 0, *picks)


def solve(field, block):
    return lax.dot_general(field.astype(jnp.bfloat16), block, (((1,), (1,)), ((), ())), preferred_element_type=jnp.float32)


def remote_terms(core, own, table, x_of, block_of, mine, theirs, local=None):
    for p in range(len(FACES)):
        for other, out in ((True, theirs[p]), (False, mine[p])):
            face = face_of(p, 1 - core if other else core, own)
            count = table[0, COUNTS + face]
            for s in range(CAP // 2):
                terms = []
                for slot in (s, s + CAP // 2):
                    at = jnp.minimum(slot, count - 1)
                    entry = table[0, face * STRIDE + at]
                    terms.append(jnp.dot(x_of(entry), block_of(face, at, entry), preferred_element_type=jnp.float32))
                    out[slot * ADJ : (slot + 1) * ADJ] = terms[-1][:, 0:128].astype(out.dtype)
                    if local is not None and not other:
                        label = jnp.where(slot < count, local[face, entry] + 1, 0)
                        out[BODY + slot : BODY + slot + 1] = jnp.full((1, 128), label, jnp.int32).astype(jnp.float32)
                both = jnp.concatenate([terms[0][:, 128:WIDTH], terms[1][:, 128:WIDTH]], axis=1)
                out[WIDE + s * ADJ : WIDE + (s + 1) * ADJ] = both.astype(out.dtype)
            if local is not None and other:
                out[BODY:] = jnp.zeros((CAP, 128), out.dtype)


def first_kernel(off, precond, rhs, owner, local, x_half, xb, pre_v, table, m0, m1, m2, t0, t1, t2,
                 blocks, rhs_v, owner_s, local_s, sems, pre_sem, small_sems):
    core, own = lax.axis_index("blk"), lax.axis_index("rows")
    copies = [pltpu.make_async_copy(a, b, small_sems.at[k]) for k, (a, b) in enumerate(((owner, owner_s), (local, local_s), (rhs, rhs_v)))]
    for copy in copies:
        copy.start()
    pre_copy = pltpu.make_async_copy(precond, pre_v, pre_sem)
    pre_copy.start()
    copies[0].wait()

    def fetch(face, slot, entry):
        return pltpu.make_async_copy(off.at[entry, face], blocks.at[face * CAP + slot], sems.at[face * CAP + slot])

    def list_row(i, ranks):
        after = []
        for k in range(FAN):
            remote = owner_s[k, i] != own
            rank = ranks[k]
            table[0, k * STRIDE + rank] = i

            @pl.when(remote)
            def _():
                fetch(k, rank, i).start()

            after.append(rank + remote.astype(jnp.int32))
        return tuple(after)

    counts = lax.fori_loop(0, ROWS, list_row, (jnp.int32(0),) * FAN)
    for k in range(FAN):
        table[0, COUNTS + k] = counts[k]
    copies[1].wait()
    copies[2].wait()
    pre_copy.wait()

    def row(n, _):
        x = solve(rhs_v[n], pre_v[n])
        x_half[n] = x
        xb[n] = x.astype(jnp.bfloat16)
        return 0

    lax.fori_loop(0, ROWS, row, 0, unroll=4)

    for k in range(FAN):
        def arrive(slot, _):
            fetch(k, slot, 0).wait()
            return 0

        lax.fori_loop(0, counts[k], arrive, 0)
    remote_terms(core, own, table, lambda e: xb[e], lambda face, at, e: blocks[face * CAP + at], (m0, m1, m2), (t0, t1, t2), local_s)


def local_terms(first, last, own, xb, off_v, diag_v, owner, local, sums):
    def row(i, _):
        x = xb[i]
        places, terms = [i], [jnp.dot(x, diag_v[i], preferred_element_type=jnp.float32)]
        for k in range(FAN):
            places.append(jnp.where(owner[k, i] == own, local[k, i], ROWS))
            terms.append(jnp.dot(x, off_v[i, k], preferred_element_type=jnp.float32))
        for place, term in zip(places, terms):
            sums[place] = sums[place] + term
        return 0

    lax.fori_loop(first, last, row, 0, unroll=True if last - first <= 4 else 4)


def first_local_kernel(off, diag, xb, owner, local, off_v, diag_v, *rest):
    partial, (sums, owner_s, local_s, sems, small_sems) = rest[:PIECES], rest[PIECES:]
    own = lax.axis_index("rows")
    small = [pltpu.make_async_copy(a, b, small_sems.at[k]) for k, (a, b) in enumerate(((owner, owner_s), (local, local_s)))]
    for copy in small:
        copy.start()
    copies = []
    for chunk in range(CHUNKS):
        part = pl.ds(chunk * PER, PER)
        copies.append([pltpu.make_async_copy(a.at[part], b.at[part], sems.at[k, chunk]) for k, (a, b) in enumerate(((off, off_v), (diag, diag_v)))])
        for copy in copies[-1]:
            copy.start()
    sums[...] = jnp.zeros(sums.shape, sums.dtype)
    for copy in small:
        copy.wait()
    for chunk in range(CHUNKS):
        for copy in copies[chunk]:
            copy.wait()
        local_terms(chunk * PER, (chunk + 1) * PER, own, xb, off_v, diag_v, owner_s, local_s, sums)
    for piece in range(PIECES):
        partial[piece][...] = sums[piece * PIECE : (piece + 1) * PIECE]


def place(messages, label_of, first, narrow_sum, wide_sum):
    wide_sum[...] = jnp.zeros(wide_sum.shape, wide_sum.dtype)
    narrow_sum[...] = jnp.zeros(narrow_sum.shape, narrow_sum.dtype)
    lane = lax.broadcasted_iota(jnp.int32, (ADJ, 128), 1)
    for p, message in enumerate(messages):
        for s in range(CAP // 2):
            at = []
            for slot in (s, s + CAP // 2):
                label = label_of(first + p * CAP + slot)
                at.append(jnp.where(label == 0, ROWS, label - 1))
                wide_sum[at[-1]] += message[slot * ADJ : (slot + 1) * ADJ].astype(jnp.float32)
            both = message[WIDE + s * ADJ : WIDE + (s + 1) * ADJ].astype(jnp.float32)
            narrow_sum[at[0]] += jnp.where(lane < 64, both, 0.0)
            narrow_sum[at[1]] += jnp.where(lane < 64, 0.0, both)


def read_labels(messages, row_v, labels_s, sem):
    found = jnp.concatenate([m[BODY:].astype(jnp.float32) for m in messages], axis=0)
    rows = lax.broadcasted_iota(jnp.int32, found.shape, 0)
    lanes = lax.broadcasted_iota(jnp.int32, found.shape, 1)
    row = jnp.sum(jnp.where(rows == lanes, found, 0.0), axis=0, keepdims=True)
    row_v[...] = row.astype(jnp.int32)
    copy = pltpu.make_async_copy(row_v, labels_s, sem)
    copy.start()
    return copy


def residual_of(n, rhs, ours, other, piece, wides, narrows):
    narrow = narrows[0][n] + narrows[1][n]
    narrow = narrow + pltpu.roll(narrow, 64, 1)
    got = jnp.concatenate([wides[0][n] + wides[1][n], narrow[:, 0:64]], axis=1)
    return rhs[n] - ((ours[n - piece * PIECE] + other[n - piece * PIECE]) + got)


def middle_kernel(off_v, pre_v, rhs, table, x_before, *rest):
    ours, others, rest = rest[:PIECES], rest[PIECES : 2 * PIECES], rest[2 * PIECES :]
    middle_body(off_v, pre_v, rhs, table, x_before, ours, others, *rest)


def middle_body(off_v, pre_v, rhs, table, x_before, ours, other, g0, g1, g2, f0, f1, f2,
                  vb, xb, labels_out, m0, m1, m2, t0, t1, t2,
                  wide_a, wide_b, narrow_a, narrow_b, row_v, label_sem):
    core, own = lax.axis_index("blk"), lax.axis_index("rows")
    read_labels((g0, g1, g2, f0, f1, f2), row_v, labels_out, label_sem).wait()
    label_of = lambda at: labels_out[0, at]
    place((g0, g1, g2), label_of, 0, narrow_a, wide_a)
    place((f0, f1, f2), label_of, 3 * CAP, narrow_b, wide_b)

    for piece in range(PIECES):
        def row(n, _):
            left = residual_of(n, rhs, ours[piece], other[piece], piece, (wide_a, wide_b), (narrow_a, narrow_b)).astype(jnp.bfloat16)
            vb[n] = left
            xb[n] = (x_before[n] + solve(left, pre_v[n])).astype(jnp.bfloat16)
            return 0

        lax.fori_loop(piece * PIECE, (piece + 1) * PIECE, row, 0, unroll=4)
    remote_terms(core, own, table, lambda e: xb[e], lambda face, at, e: off_v[e, face], (m0, m1, m2), (t0, t1, t2))


def middle_local_kernel(off_v, diag_v, xb, owner, local, *rest):
    partial, sums = rest[:PIECES], rest[PIECES]
    own = lax.axis_index("rows")
    sums[...] = jnp.zeros(sums.shape, sums.dtype)
    local_terms(0, ROWS, own, xb, off_v, diag_v, owner, local, sums)
    for piece in range(PIECES):
        partial[piece][...] = sums[piece * PIECE : (piece + 1) * PIECE]


def last_kernel(pre_v, pre_other, rhs, vb, *rest):
    ours, others, rest = rest[:PIECES], rest[PIECES : 2 * PIECES], rest[2 * PIECES :]
    last_body(pre_v, pre_other, rhs, vb, ours, others, *rest)


def last_body(pre_v, pre_other, rhs, vb, ours, other, labels, g0, g1, g2, f0, f1, f2,
              adjoint, residual, wide_a, wide_b, narrow_a, narrow_b):
    core = lax.axis_index("blk")
    label_of = lambda at: labels[0, at]
    place((g0, g1, g2), label_of, 0, narrow_a, wide_a)
    place((f0, f1, f2), label_of, 3 * CAP, narrow_b, wide_b)

    for piece in range(PIECES):
        def row(n, _):
            left = residual_of(n, rhs, ours[piece], other[piece], piece, (wide_a, wide_b), (narrow_a, narrow_b))
            residual[n] = left
            fields = jnp.concatenate([rhs[n].astype(jnp.bfloat16), vb[n], left.astype(jnp.bfloat16)], axis=0)
            halves = [solve(fields, pre[n]) for pre in (pre_v, pre_other)]
            mine, theirs = [(half[0:ADJ] + half[ADJ : 2 * ADJ]) + half[2 * ADJ :] for half in halves]
            adjoint[n, :, 0:HALF] = jnp.where(core == 0, mine, theirs)
            adjoint[n, :, HALF:WIDTH] = jnp.where(core == 0, theirs, mine)
            return 0

        lax.fori_loop(piece * PIECE, (piece + 1) * PIECE, row, 0, unroll=4)


def call(kernel, name, out_shape, in_specs, out_specs, scratch_shapes, cost=None):
    params = pltpu.CompilerParams(vmem_limit_bytes=VMEM_LIMIT)
    return pl.pallas_call(kernel, out_shape=out_shape, in_specs=in_specs, out_specs=out_specs, scratch_shapes=scratch_shapes,
                          compiler_params=params, cost_estimate=cost, name=name)


def on_device(off_blocks, diag_blocks, precond, adj_rhs, col_owner, col_local):
    nrows = lax.axis_size("rows")
    offsets = (1, nrows - 1, 2, nrows - 2, nrows // 2, nrows // 2 + 1)
    shape, f32, bf16, i32 = jax.ShapeDtypeStruct, jnp.float32, jnp.bfloat16, jnp.int32
    field, half_blocks = shape((ROWS, ADJ, WIDTH), f32), shape((ROWS, HALF, WIDTH), bf16)
    pieces = [shape((PIECE, ADJ, WIDTH), f32)] * PIECES
    row_of_ints = shape((1, 128), i32)
    dma = pltpu.SemaphoreType.DMA

    def across(x):
        return lax.ppermute(x, "blk", [(0, 1), (1, 0)])

    def to_faces(x, p):
        pairs = [(2 * i + c, 2 * ((i + offsets[FACES[ORDER[p]][c][i % 4]]) % nrows) + c) for i in range(nrows) for c in range(2)]
        return lax.ppermute(x, ("rows", "blk"), pairs)

    def exchange(mine, theirs, *later):
        sums = [(m + across(t).astype(f32)).astype(bf16) for m, t in zip(mine, theirs)]
        got = [to_faces(x, p) for p, x in enumerate(sums)]
        later = lax.optimization_barrier((*sums, *later))[len(sums) :]
        return got, *later

    def tie(x, *others):
        return lax.optimization_barrier((x, *others))

    def hand_on(got, parts):
        got[0], *parts = tie(got[0], *parts)
        got[1] = tie(got[1], parts[0])[0]
        got[2] = tie(got[2], parts[0])[0]
        return parts, [across(x) for x in parts], got, [across(g) for g in got]

    def in_hbm(*arrays):
        return [pltpu.with_memory_space_constraint(x, pltpu.HBM) for x in arrays]

    cost = pl.CostEstimate(flops=2 * ROWS * (FAN + 1) * ADJ * HALF * WIDTH, bytes_accessed=40_000_000, transcendentals=0)
    ints = [pltpu.SMEM((FAN, ROWS), i32)] * 2
    received = [pltpu.VMEM((ROWS + 1, ADJ, 128), f32)] * 4
    sums = pltpu.VMEM((ROWS + 1, ADJ, WIDTH), f32)
    owner, local = col_owner.T, col_local.T

    x_half, xb, pre_v, table, *messages = call(
        first_kernel,
        "first_remote_terms",
        [shape((ROWS, ADJ, HALF), f32), shape((ROWS, ADJ, HALF), bf16), half_blocks, row_of_ints]
        + [shape((BODY + CAP, 128), f32)] * 3 + [shape((BODY + CAP, 128), bf16)] * 3,
        [HBM] * 5,
        [VM, VM, VM, SM] + [VM] * 6,
        [pltpu.VMEM((FAN * CAP, HALF, WIDTH), bf16), pltpu.VMEM((ROWS, ADJ, WIDTH), f32)] + ints + [dma((FAN * CAP,)), dma, dma((3,))],
    )(*in_hbm(off_blocks, precond, adj_rhs, owner, local))
    got, xb, pre_v = exchange(messages[:3], messages[3:], xb, pre_v)
    off_v, diag_v, *partial = call(
        first_local_kernel,
        "first_local_terms",
        [shape((ROWS, FAN, HALF, WIDTH), bf16), half_blocks] + pieces,
        [HBM, HBM, VM, HBM, HBM],
        [VM] * (2 + PIECES),
        [sums] + ints + [dma((2, CHUNKS)), dma((2,))],
        cost,
    )(*in_hbm(off_blocks, diag_blocks), xb, *in_hbm(owner, local))
    partial, other, got, forwarded = hand_on(got, partial)
    pre_other, got[1] = tie(across(pre_v), got[1])

    vb, xb, labels, *messages = call(
        middle_kernel,
        "middle_remote_terms",
        [shape((ROWS, ADJ, WIDTH), bf16), shape((ROWS, ADJ, HALF), bf16), row_of_ints]
        + [shape((BODY, 128), f32)] * 3 + [shape((BODY, 128), bf16)] * 3,
        [VM, VM, VM, SM, VM] + [VM] * (2 * PIECES + 6),
        [VM, VM, SM] + [VM] * 6,
        received + [pltpu.VMEM((1, 128), i32), dma],
    )(off_v, pre_v, adj_rhs, table, x_half, *partial, *other, *got, *forwarded)
    got, xb = exchange(messages[:3], messages[3:], xb)
    partial = call(
        middle_local_kernel,
        "middle_local_terms",
        pieces,
        [VM, VM, VM, SM, SM],
        [VM] * PIECES,
        [sums],
        cost,
    )(off_v, diag_v, xb, owner, local)
    partial, other, got, forwarded = hand_on(got, partial)

    return call(
        last_kernel,
        "last_terms",
        [field, field],
        [VM] * (4 + 2 * PIECES) + [SM] + [VM] * 6,
        [VM] * 2,
        received,
    )(pre_v, pre_other, adj_rhs, vb, *partial, *other, labels, *got, *forwarded)


def solution(mesh):
    in_specs = (
        P("rows", None, "blk", None),
        P("rows", "blk", None),
        P("rows", "blk", None),
        P("rows", None, None),
        P("rows", None),
        P("rows", None),
    )
    out_specs = (P("rows", None, None), P("rows", None, None))

    def program(*arrays):
        return tuple(on_device(*arrays))

    return jax.shard_map(program, mesh=mesh, in_specs=in_specs, out_specs=out_specs, check_vma=False)
```

```python
import jax
import jax.numpy as jnp
from jax import lax
from jax.experimental import pallas as pl
from jax.experimental.pallas import tpu as pltpu
from jax.sharding import PartitionSpec as P

ROWS = 32
FAN = 6
ADJ = 16
WIDTH = 192
HALF = 96
CAP = 16
WIDE = CAP * ADJ
BODY = WIDE + WIDE // 2
NEAR, SEAM, FAR = 0, 1, 2
ORDER = (SEAM, FAR, NEAR)
FACES = (
    ((0, 1, 0, 1), (2, 2, 3, 3)),
    ((1, 0, 1, 0), (3, 3, 2, 2)),
    ((4, 4, 4, 4), (5, 5, 5, 5)),
)
STRIDE = CAP + 1
COUNTS = FAN * STRIDE
CHUNKS = 8
PIECES = 2
TIE = 1
PARTS = 4
UNROLL = 32
LOCAL_UNROLL = 16
PIECE = ROWS // PIECES
PER = ROWS // CHUNKS
VMEM_LIMIT = 24 * 1024 * 1024

VM = pl.BlockSpec(memory_space=pltpu.VMEM)
SM = pl.BlockSpec(memory_space=pltpu.SMEM)
ANY = pl.BlockSpec(memory_space=pl.ANY)
HBM = pl.BlockSpec(memory_space=pltpu.HBM)


def face_of(p, core, own):
    kind = lax.rem(own, 4)
    picks = []
    for faces in FACES[ORDER[p]]:
        pick = faces[3]
        for k in (2, 1, 0):
            pick = jnp.where(kind == k, faces[k], pick)
        picks.append(pick)
    return jnp.where(core == 0, *picks)


def solve(field, block):
    return lax.dot_general(field.astype(jnp.bfloat16), block, (((1,), (1,)), ((), ())), preferred_element_type=jnp.float32)


def faces_in_order(core, own):
    return [face_of(p, 1 - core if other else core, own) for p in range(len(FACES)) for other in (True, False)]


def remote_terms(core, own, table, x_of, block_of, mine, theirs, local=None):
    faces = faces_in_order(core, own)
    for p in range(len(FACES)):
        for other, out in ((True, theirs[p]), (False, mine[p])):
            face = faces[2 * p + (0 if other else 1)]
            count = table[0, COUNTS + face]
            for s in range(CAP // 2):
                terms = []
                for slot in (s, s + CAP // 2):
                    at = jnp.minimum(slot, count - 1)
                    entry = table[0, face * STRIDE + at]
                    terms.append(jnp.dot(x_of(entry), block_of(face, at, entry), preferred_element_type=jnp.float32))
                    out[slot * ADJ : (slot + 1) * ADJ] = terms[-1][:, 0:128].astype(out.dtype)
                    if local is not None and not other:
                        label = jnp.where(slot < count, local[face, entry] + 1, 0)
                        out[BODY + slot : BODY + slot + 1] = jnp.full((1, 128), label, jnp.int32).astype(jnp.float32)
                both = jnp.concatenate([terms[0][:, 128:WIDTH], terms[1][:, 128:WIDTH]], axis=1)
                out[WIDE + s * ADJ : WIDE + (s + 1) * ADJ] = both.astype(out.dtype)
            if local is not None and other:
                out[BODY:] = jnp.zeros((CAP, 128), out.dtype)


def list_face(face, own, owner, table):
    def entry(i, rank):
        table[0, face * STRIDE + rank] = i
        return rank + (owner[face, i] != own).astype(jnp.int32)

    table[0, COUNTS + face] = lax.fori_loop(0, ROWS, entry, jnp.int32(0), unroll=8)


def first_kernel(off, precond, rhs, owner, local, x_half, xb, pre_v, m0, m1, m2, t0, t1, t2,
                 blocks, rhs_v, owner_s, local_s, table, sems, pre_sem, small_sems):
    core, own = lax.axis_index("blk"), lax.axis_index("rows")
    copies = [pltpu.make_async_copy(a, b, small_sems.at[k]) for k, (a, b) in enumerate(((owner, owner_s), (local, local_s), (rhs, rhs_v)))]
    copies.append(pltpu.make_async_copy(precond, pre_v, pre_sem))
    for copy in copies:
        copy.start()
    copies[0].wait()

    def fetch(face, slot, entry):
        return pltpu.make_async_copy(off.at[entry, face], blocks.at[face * CAP + slot], sems.at[face * CAP + slot])

    def list_row(i, ranks):
        after = []
        for k in range(FAN):
            remote, rank = owner_s[k, i] != own, ranks[k]
            table[0, k * STRIDE + rank] = i

            @pl.when(remote)
            def _():
                fetch(k, rank, i).start()

            after.append(rank + remote.astype(jnp.int32))
        return tuple(after)

    counts = lax.fori_loop(0, ROWS, list_row, (jnp.int32(0),) * FAN, unroll=4)
    for k in range(FAN):
        table[0, COUNTS + k] = counts[k]
    for copy in copies[1:]:
        copy.wait()

    def row(n, _):
        x = solve(rhs_v[n], pre_v[n])
        x_half[n] = x
        xb[n] = x.astype(jnp.bfloat16)
        return 0

    lax.fori_loop(0, ROWS, row, 0, unroll=UNROLL)
    for k in range(FAN):
        for slot in range(CAP):

            @pl.when(slot < counts[k])
            def _():
                fetch(k, slot, 0).wait()

    remote_terms(core, own, table, lambda e: xb[e], lambda face, at, e: blocks[face * CAP + at], (m0, m1, m2), (t0, t1, t2), local_s)


def local_terms(first, last, own, xb, off_v, diag_v, owner, local, sums):
    def row(i, _):
        x = xb[i]
        places, terms = [i], [jnp.dot(x, diag_v[i], preferred_element_type=jnp.float32)]
        for k in range(FAN):
            places.append(jnp.where(owner[k, i] == own, local[k, i], ROWS))
            terms.append(jnp.dot(x, off_v[i, k], preferred_element_type=jnp.float32))
        for place, term in zip(places, terms):
            sums[place] = sums[place] + term
        return 0

    lax.fori_loop(first, last, row, 0, unroll=min(last - first, LOCAL_UNROLL))


def first_local_kernel(off, diag, xb, owner, local, off_v, diag_v, table, *rest):
    partial, (sums, owner_s, local_s, sems, small_sems) = rest[:PIECES], rest[PIECES:]
    own = lax.axis_index("rows")
    small = [pltpu.make_async_copy(a, b, small_sems.at[k]) for k, (a, b) in enumerate(((owner, owner_s), (local, local_s)))]
    for copy in small:
        copy.start()
    copies = []
    for chunk in range(CHUNKS):
        part = pl.ds(chunk * PER, PER)
        copies.append([pltpu.make_async_copy(a.at[part], b.at[part], sems.at[k, chunk]) for k, (a, b) in enumerate(((off, off_v), (diag, diag_v)))])
        for copy in copies[-1]:
            copy.start()
    sums[...] = jnp.zeros(sums.shape, sums.dtype)
    for copy in small:
        copy.wait()
    for face in range(FAN):
        list_face(face, own, owner_s, table)
    for chunk in range(CHUNKS):
        for copy in copies[chunk]:
            copy.wait()
        local_terms(chunk * PER, (chunk + 1) * PER, own, xb, off_v, diag_v, owner_s, local_s, sums)
    for piece in range(PIECES):
        partial[piece][...] = sums[piece * PIECE : (piece + 1) * PIECE]


def place(messages, label_of, first, narrow_sum, wide_sum):
    lane = lax.broadcasted_iota(jnp.int32, (ADJ, 128), 1)
    for p, message in enumerate(messages):
        for s in range(CAP // 2):
            at = []
            for slot in (s, s + CAP // 2):
                label = label_of(first + p * CAP + slot)
                at.append(jnp.where(label == 0, ROWS, label - 1))
                wide_sum[at[-1]] += message[slot * ADJ : (slot + 1) * ADJ].astype(jnp.float32)
            both = message[WIDE + s * ADJ : WIDE + (s + 1) * ADJ].astype(jnp.float32)
            narrow_sum[at[0]] += jnp.where(lane < 64, both, 0.0)
            narrow_sum[at[1]] += jnp.where(lane < 64, 0.0, both)


def gather_labels(messages, row):
    found = jnp.concatenate([m[BODY:].astype(jnp.float32) for m in messages], axis=0)
    rows = lax.broadcasted_iota(jnp.int32, found.shape, 0)
    lanes = lax.broadcasted_iota(jnp.int32, found.shape, 1)
    row[...] = jnp.sum(jnp.where(rows == lanes, found, 0.0), axis=0, keepdims=True).astype(jnp.int32)


def receive(labels_copy, labels_s, messages, ours, other, both, wides, narrows):
    for ref in (*wides, *narrows):
        ref[...] = jnp.zeros(ref.shape, ref.dtype)
    for piece in range(PIECES):
        both[piece * PIECE : (piece + 1) * PIECE] = ours[piece][...] + other[piece][...]
    labels_copy.wait()
    label_of = lambda at: labels_s[0, at]
    place(messages[:3], label_of, 0, narrows[0], wides[0])
    place(messages[3:], label_of, 3 * CAP, narrows[1], wides[1])


def residual_of(n, rhs, both, wides, narrows):
    narrow = narrows[0][n] + narrows[1][n]
    narrow = narrow + pltpu.roll(narrow, 64, 1)
    got = jnp.concatenate([wides[0][n] + wides[1][n], narrow[:, 0:64]], axis=1)
    return rhs[n] - (both[n] + got)


def middle_kernel(off_v, pre_v, rhs, table, x_before, *rest):
    ours, others, messages, rest = rest[:PIECES], rest[PIECES : 2 * PIECES], rest[2 * PIECES : 2 * PIECES + 6], rest[2 * PIECES + 6 :]
    vb, xb, labels, m0, m1, m2, t0, t1, t2, both, wide_a, wide_b, narrow_a, narrow_b, table_s, labels_s, sems = rest
    core, own = lax.axis_index("blk"), lax.axis_index("rows")
    table_copy = pltpu.make_async_copy(table, table_s, sems.at[0])
    table_copy.start()
    gather_labels(messages, labels)
    labels_copy = pltpu.make_async_copy(labels, labels_s, sems.at[1])
    labels_copy.start()
    wides, narrows = (wide_a, wide_b), (narrow_a, narrow_b)
    receive(labels_copy, labels_s, messages, ours, others, both, wides, narrows)

    def row(n, _):
        left = residual_of(n, rhs, both, wides, narrows).astype(jnp.bfloat16)
        vb[n] = left
        xb[n] = (x_before[n] + solve(left, pre_v[n])).astype(jnp.bfloat16)
        return 0

    lax.fori_loop(0, ROWS, row, 0, unroll=UNROLL)
    table_copy.wait()
    remote_terms(core, own, table_s, lambda e: xb[e], lambda face, at, e: off_v[e, face], (m0, m1, m2), (t0, t1, t2))


def middle_local_kernel(off_v, diag_v, xb, owner, local, *rest):
    partial, sums = rest[:PIECES], rest[PIECES]
    own = lax.axis_index("rows")
    sums[...] = jnp.zeros(sums.shape, sums.dtype)
    local_terms(0, ROWS, own, xb, off_v, diag_v, owner, local, sums)
    for piece in range(PIECES):
        partial[piece][...] = sums[piece * PIECE : (piece + 1) * PIECE]


def last_kernel(pre_v, pre_other, rhs, vb, *rest):
    ours, others, rest = rest[:PIECES], rest[PIECES : 2 * PIECES], rest[2 * PIECES :]
    labels, messages, rest = rest[0], rest[1:7], rest[7:]
    adjoint, residual, adjoint_v, residual_v, both, wide_a, wide_b, narrow_a, narrow_b, labels_s, label_sem, sems = rest
    core = lax.axis_index("blk")
    labels_copy = pltpu.make_async_copy(labels, labels_s, label_sem)
    labels_copy.start()
    wides, narrows = (wide_a, wide_b), (narrow_a, narrow_b)
    receive(labels_copy, labels_s, messages, ours, others, both, wides, narrows)

    def row(n, _):
        left = residual_of(n, rhs, both, wides, narrows)
        residual_v[n] = left
        fields = jnp.concatenate([rhs[n].astype(jnp.bfloat16), vb[n], left.astype(jnp.bfloat16)], axis=0)
        halves = [solve(fields, blocks[n]) for blocks in (pre_v, pre_other)]
        mine, theirs = [(half[0:ADJ] + half[ADJ : 2 * ADJ]) + half[2 * ADJ :] for half in halves]
        adjoint_v[n, :, 0:HALF] = jnp.where(core == 0, mine, theirs)
        adjoint_v[n, :, HALF:WIDTH] = jnp.where(core == 0, theirs, mine)
        return 0

    copies = []
    for piece in range(PARTS):
        rows = pl.ds(piece * (ROWS // PARTS), ROWS // PARTS)
        lax.fori_loop(piece * (ROWS // PARTS), (piece + 1) * (ROWS // PARTS), row, 0, unroll=True)
        for k, (a, b) in enumerate(((residual_v, residual), (adjoint_v, adjoint))):
            copies.append(pltpu.make_async_copy(a.at[rows], b.at[rows], sems.at[k, piece]))
            copies[-1].start()
    for copy in copies:
        copy.wait()


def call(kernel, name, out_shape, in_specs, out_specs, scratch_shapes, cost=None):
    params = pltpu.CompilerParams(vmem_limit_bytes=VMEM_LIMIT)
    return pl.pallas_call(kernel, out_shape=out_shape, in_specs=in_specs, out_specs=out_specs, scratch_shapes=scratch_shapes,
                          compiler_params=params, cost_estimate=cost, name=name)


def on_device(off_blocks, diag_blocks, precond, adj_rhs, col_owner, col_local):
    nrows = lax.axis_size("rows")
    offsets = (1, nrows - 1, 2, nrows - 2, nrows // 2, nrows // 2 + 1)
    shape, f32, bf16, i32 = jax.ShapeDtypeStruct, jnp.float32, jnp.bfloat16, jnp.int32
    field, half_blocks = shape((ROWS, ADJ, WIDTH), f32), shape((ROWS, HALF, WIDTH), bf16)
    pieces = [shape((PIECE, ADJ, WIDTH), f32)] * PIECES
    row_of_ints = shape((1, 128), i32)
    dma = pltpu.SemaphoreType.DMA

    def across(x):
        return lax.ppermute(x, "blk", [(0, 1), (1, 0)])

    def to_faces(x, p):
        pairs = [(2 * i + c, 2 * ((i + offsets[FACES[ORDER[p]][c][i % 4]]) % nrows) + c) for i in range(nrows) for c in range(2)]
        return lax.ppermute(x, ("rows", "blk"), pairs)

    def tie(*arrays):
        return lax.optimization_barrier(arrays)

    def exchange(mine, theirs, *later, chain=False):
        sums = []
        for m, t in zip(mine, theirs):
            if sums and chain:
                t, sums[0] = tie(t, sums[0])
            sums.append((m + across(t).astype(f32)).astype(bf16))
        got = [to_faces(x, p) for p, x in enumerate(sums)]
        later = lax.optimization_barrier((*sums, *later))[len(sums) :]
        return got, *later

    def hand_on(got, parts):
        for p in range(len(FACES)):
            if p == TIE:
                got[p], parts[0] = tie(got[p], parts[0])
            else:
                got[p] = tie(got[p], parts[0])[0]
        return parts, [across(x) for x in parts], got, [across(g) for g in got]

    def in_hbm(*arrays):
        return [pltpu.with_memory_space_constraint(x, pltpu.HBM) for x in arrays]

    cost = pl.CostEstimate(flops=2 * ROWS * (FAN + 1) * ADJ * HALF * WIDTH, bytes_accessed=40_000_000, transcendentals=0)
    ints = [pltpu.SMEM((FAN, ROWS), i32)] * 2
    received = [pltpu.VMEM((ROWS, ADJ, WIDTH), f32)] + [pltpu.VMEM((ROWS + 1, ADJ, 128), f32)] * 4
    sums = pltpu.VMEM((ROWS + 1, ADJ, WIDTH), f32)
    owner, local = col_owner.T, col_local.T
    pre_other = across(precond)

    x_half, xb, pre_v, *messages = call(
        first_kernel,
        "first_remote_terms",
        [shape((ROWS, ADJ, HALF), f32), shape((ROWS, ADJ, HALF), bf16), half_blocks]
        + [shape((BODY + CAP, 128), f32)] * 3 + [shape((BODY + CAP, 128), bf16)] * 3,
        [HBM] * 5,
        [VM] * 9,
        [pltpu.VMEM((FAN * CAP, HALF, WIDTH), bf16), pltpu.VMEM((ROWS, ADJ, WIDTH), f32)] + ints
        + [pltpu.SMEM((1, 128), i32), dma((FAN * CAP,)), dma, dma((3,))],
    )(*in_hbm(off_blocks, precond, adj_rhs, owner, local))
    got, xb = exchange(messages[:3], messages[3:], xb)
    xb, pre_other = tie(xb, pre_other)
    off_v, diag_v, table, *partial = call(
        first_local_kernel,
        "first_local_terms",
        [shape((ROWS, FAN, HALF, WIDTH), bf16), half_blocks, row_of_ints] + pieces,
        [HBM, HBM, VM, HBM, HBM],
        [VM] * 2 + [SM] + [VM] * PIECES,
        [sums] + ints + [dma((2, CHUNKS)), dma((2,))],
        cost,
    )(*in_hbm(off_blocks, diag_blocks), xb, *in_hbm(owner, local))
    partial, other, got, forwarded = hand_on(got, list(partial))

    vb, xb, labels, *messages = call(
        middle_kernel,
        "middle_remote_terms",
        [shape((ROWS, ADJ, WIDTH), bf16), shape((ROWS, ADJ, HALF), bf16), row_of_ints]
        + [shape((BODY, 128), f32)] * 3 + [shape((BODY, 128), bf16)] * 3,
        [VM, VM, VM, ANY, VM] + [VM] * (2 * PIECES + 6),
        [VM] * 9,
        received + [pltpu.SMEM((1, 128), i32), pltpu.SMEM((1, 128), i32), dma((2,))],
    )(off_v, pre_v, adj_rhs, table, x_half, *partial, *other, *got, *forwarded)
    got, xb = exchange(messages[:3], messages[3:], xb, chain=True)
    partial = call(
        middle_local_kernel,
        "middle_local_terms",
        pieces,
        [VM, VM, VM, SM, SM],
        [VM] * PIECES,
        [sums],
        cost,
    )(off_v, diag_v, xb, owner, local)
    partial, other, got, forwarded = hand_on(got, list(partial))

    return call(
        last_kernel,
        "last_terms",
        [field, field],
        [VM] * (4 + 2 * PIECES) + [ANY] + [VM] * 6,
        [HBM] * 2,
        [pltpu.VMEM((ROWS, ADJ, WIDTH), f32)] * 2 + received + [pltpu.SMEM((1, 128), i32), dma, dma((2, PARTS))],
    )(pre_v, pre_other, adj_rhs, vb, *partial, *other, labels, *got, *forwarded)


def solution(mesh):
    in_specs = (
        P("rows", None, "blk", None),
        P("rows", "blk", None),
        P("rows", "blk", None),
        P("rows", None, None),
        P("rows", None),
        P("rows", None),
    )
    out_specs = (P("rows", None, None), P("rows", None, None))

    def program(*arrays):
        return tuple(on_device(*arrays))

    return jax.shard_map(program, mesh=mesh, in_specs=in_specs, out_specs=out_specs, check_vma=False)
```

```python
import jax
import jax.numpy as jnp
from jax import lax
from jax.experimental import pallas as pl
from jax.experimental.pallas import tpu as pltpu
from jax.sharding import PartitionSpec as P

ROWS = 32
FAN = 6
ADJ = 16
WIDTH = 192
HALF = 96
CAP = 16
WIDE = CAP * ADJ
BODY = WIDE + WIDE // 2
NEAR, SEAM, FAR = 0, 1, 2
ORDER = (FAR, SEAM, NEAR)
FACES = (
    ((0, 1, 0, 1), (2, 2, 3, 3)),
    ((1, 0, 1, 0), (3, 3, 2, 2)),
    ((4, 4, 4, 4), (5, 5, 5, 5)),
)
STRIDE = CAP + 1
COUNTS = FAN * STRIDE
CHUNKS = 8
PIECES = 2
TIE = 0
LAST = 2
PARTS = 4
UNROLL = 32
LOCAL_UNROLL = 16
PIECE = ROWS // PIECES
PER = ROWS // CHUNKS
VMEM_LIMIT = 24 * 1024 * 1024

VM = pl.BlockSpec(memory_space=pltpu.VMEM)
SM = pl.BlockSpec(memory_space=pltpu.SMEM)
ANY = pl.BlockSpec(memory_space=pl.ANY)
HBM = pl.BlockSpec(memory_space=pltpu.HBM)


def face_of(p, core, own):
    kind = lax.rem(own, 4)
    picks = []
    for faces in FACES[ORDER[p]]:
        pick = faces[3]
        for k in (2, 1, 0):
            pick = jnp.where(kind == k, faces[k], pick)
        picks.append(pick)
    return jnp.where(core == 0, *picks)


def solve(field, block):
    return lax.dot_general(field.astype(jnp.bfloat16), block, (((1,), (1,)), ((), ())), preferred_element_type=jnp.float32)


def faces_in_order(core, own):
    return [face_of(p, 1 - core if other else core, own) for p in range(len(FACES)) for other in (True, False)]


def remote_terms(core, own, table, x_of, block_of, mine, theirs, local=None):
    faces = faces_in_order(core, own)
    for p in range(len(FACES)):
        for other, out in ((True, theirs[p]), (False, mine[p])):
            face = faces[2 * p + (0 if other else 1)]
            count = table[0, COUNTS + face]
            for s in range(CAP // 2):
                terms = []
                for slot in (s, s + CAP // 2):
                    at = jnp.minimum(slot, count - 1)
                    entry = table[0, face * STRIDE + at]
                    terms.append(jnp.dot(x_of(entry), block_of(face, at, entry), preferred_element_type=jnp.float32))
                    out[slot * ADJ : (slot + 1) * ADJ] = terms[-1][:, 0:128].astype(out.dtype)
                    if local is not None and not other:
                        label = jnp.where(slot < count, local[face, entry] + 1, 0)
                        out[BODY + slot : BODY + slot + 1] = jnp.full((1, 128), label, jnp.int32).astype(jnp.float32)
                both = jnp.concatenate([terms[0][:, 128:WIDTH], terms[1][:, 128:WIDTH]], axis=1)
                out[WIDE + s * ADJ : WIDE + (s + 1) * ADJ] = both.astype(out.dtype)
            if local is not None and other:
                out[BODY:] = jnp.zeros((CAP, 128), out.dtype)


def list_face(face, own, owner, table):
    def entry(i, rank):
        table[0, face * STRIDE + rank] = i
        return rank + (owner[face, i] != own).astype(jnp.int32)

    table[0, COUNTS + face] = lax.fori_loop(0, ROWS, entry, jnp.int32(0), unroll=8)


def first_kernel(off, precond, rhs, owner, local, x_half, xb, pre_v, m0, m1, m2, t0, t1, t2,
                 blocks, rhs_v, owner_s, local_s, table, sems, pre_sem, small_sems):
    core, own = lax.axis_index("blk"), lax.axis_index("rows")
    copies = [pltpu.make_async_copy(a, b, small_sems.at[k]) for k, (a, b) in enumerate(((owner, owner_s), (local, local_s), (rhs, rhs_v)))]
    copies.append(pltpu.make_async_copy(precond, pre_v, pre_sem))
    for copy in copies:
        copy.start()
    copies[0].wait()

    def fetch(face, slot, entry):
        return pltpu.make_async_copy(off.at[entry, face], blocks.at[face * CAP + slot], sems.at[face * CAP + slot])

    def list_row(i, ranks):
        after = []
        for k in range(FAN):
            remote, rank = owner_s[k, i] != own, ranks[k]
            table[0, k * STRIDE + rank] = i

            @pl.when(remote)
            def _():
                fetch(k, rank, i).start()

            after.append(rank + remote.astype(jnp.int32))
        return tuple(after)

    counts = lax.fori_loop(0, ROWS, list_row, (jnp.int32(0),) * FAN, unroll=4)
    for k in range(FAN):
        table[0, COUNTS + k] = counts[k]
    for copy in copies[1:]:
        copy.wait()

    def row(n, _):
        x = solve(rhs_v[n], pre_v[n])
        x_half[n] = x
        xb[n] = x.astype(jnp.bfloat16)
        return 0

    lax.fori_loop(0, ROWS, row, 0, unroll=UNROLL)
    for k in range(FAN):
        for slot in range(CAP):

            @pl.when(slot < counts[k])
            def _():
                fetch(k, slot, 0).wait()

    remote_terms(core, own, table, lambda e: xb[e], lambda face, at, e: blocks[face * CAP + at], (m0, m1, m2), (t0, t1, t2), local_s)


def local_terms(first, last, own, xb, off_v, diag_v, owner, local, sums):
    def row(i, _):
        x = xb[i]
        places, terms = [i], [jnp.dot(x, diag_v[i], preferred_element_type=jnp.float32)]
        for k in range(FAN):
            places.append(jnp.where(owner[k, i] == own, local[k, i], ROWS))
            terms.append(jnp.dot(x, off_v[i, k], preferred_element_type=jnp.float32))
        for place, term in zip(places, terms):
            sums[place] = sums[place] + term
        return 0

    lax.fori_loop(first, last, row, 0, unroll=min(last - first, LOCAL_UNROLL))


def first_local_kernel(off, diag, xb, owner, local, off_v, diag_v, table, *rest):
    partial, (sums, owner_s, local_s, sems, small_sems) = rest[:PIECES], rest[PIECES:]
    own = lax.axis_index("rows")
    small = [pltpu.make_async_copy(a, b, small_sems.at[k]) for k, (a, b) in enumerate(((owner, owner_s), (local, local_s)))]
    for copy in small:
        copy.start()
    copies = []
    for chunk in range(CHUNKS):
        part = pl.ds(chunk * PER, PER)
        copies.append([pltpu.make_async_copy(a.at[part], b.at[part], sems.at[k, chunk]) for k, (a, b) in enumerate(((off, off_v), (diag, diag_v)))])
        for copy in copies[-1]:
            copy.start()
    sums[...] = jnp.zeros(sums.shape, sums.dtype)
    for copy in small:
        copy.wait()
    for face in range(FAN):
        list_face(face, own, owner_s, table)
    for chunk in range(CHUNKS):
        for copy in copies[chunk]:
            copy.wait()
        local_terms(chunk * PER, (chunk + 1) * PER, own, xb, off_v, diag_v, owner_s, local_s, sums)
    for piece in range(PIECES):
        partial[piece][...] = sums[piece * PIECE : (piece + 1) * PIECE]


def place(messages, label_of, first, narrow_sum, wide_sum):
    lane = lax.broadcasted_iota(jnp.int32, (ADJ, 128), 1)
    for p, message in enumerate(messages):
        for s in range(CAP // 2):
            at = []
            for slot in (s, s + CAP // 2):
                label = label_of(first + p * CAP + slot)
                at.append(jnp.where(label == 0, ROWS, label - 1))
                wide_sum[at[-1]] += message[slot * ADJ : (slot + 1) * ADJ].astype(jnp.float32)
            both = message[WIDE + s * ADJ : WIDE + (s + 1) * ADJ].astype(jnp.float32)
            narrow_sum[at[0]] += jnp.where(lane < 64, both, 0.0)
            narrow_sum[at[1]] += jnp.where(lane < 64, 0.0, both)


def gather_labels(messages, row):
    found = jnp.concatenate([m[BODY:].astype(jnp.float32) for m in messages], axis=0)
    rows = lax.broadcasted_iota(jnp.int32, found.shape, 0)
    lanes = lax.broadcasted_iota(jnp.int32, found.shape, 1)
    row[...] = jnp.sum(jnp.where(rows == lanes, found, 0.0), axis=0, keepdims=True).astype(jnp.int32)


def receive(labels_copy, labels_s, messages, ours, other, both, wides, narrows):
    for ref in (*wides, *narrows):
        ref[...] = jnp.zeros(ref.shape, ref.dtype)
    for piece in range(PIECES):
        both[piece * PIECE : (piece + 1) * PIECE] = ours[piece][...] + other[piece][...]
    labels_copy.wait()
    label_of = lambda at: labels_s[0, at]
    place(messages[:3], label_of, 0, narrows[0], wides[0])
    place(messages[3:], label_of, 3 * CAP, narrows[1], wides[1])


def residual_of(n, rhs, both, wides, narrows):
    narrow = narrows[0][n] + narrows[1][n]
    narrow = narrow + pltpu.roll(narrow, 64, 1)
    got = jnp.concatenate([wides[0][n] + wides[1][n], narrow[:, 0:64]], axis=1)
    return rhs[n] - (both[n] + got)


def middle_kernel(off_v, pre_v, rhs, table, x_before, *rest):
    ours, others, messages, rest = rest[:PIECES], rest[PIECES : 2 * PIECES], rest[2 * PIECES : 2 * PIECES + 6], rest[2 * PIECES + 6 :]
    vb, xb, labels, m0, m1, m2, t0, t1, t2, both, wide_a, wide_b, narrow_a, narrow_b, table_s, labels_s, sems = rest
    core, own = lax.axis_index("blk"), lax.axis_index("rows")
    table_copy = pltpu.make_async_copy(table, table_s, sems.at[0])
    table_copy.start()
    gather_labels(messages, labels)
    labels_copy = pltpu.make_async_copy(labels, labels_s, sems.at[1])
    labels_copy.start()
    wides, narrows = (wide_a, wide_b), (narrow_a, narrow_b)
    receive(labels_copy, labels_s, messages, ours, others, both, wides, narrows)

    def row(n, _):
        left = residual_of(n, rhs, both, wides, narrows).astype(jnp.bfloat16)
        vb[n] = left
        xb[n] = (x_before[n] + solve(left, pre_v[n])).astype(jnp.bfloat16)
        return 0

    lax.fori_loop(0, ROWS, row, 0, unroll=UNROLL)
    table_copy.wait()
    remote_terms(core, own, table_s, lambda e: xb[e], lambda face, at, e: off_v[e, face], (m0, m1, m2), (t0, t1, t2))


def middle_local_kernel(off_v, diag_v, xb, owner, local, *rest):
    partial, sums = rest[:PIECES], rest[PIECES]
    own = lax.axis_index("rows")
    sums[...] = jnp.zeros(sums.shape, sums.dtype)
    local_terms(0, ROWS, own, xb, off_v, diag_v, owner, local, sums)
    for piece in range(PIECES):
        partial[piece][...] = sums[piece * PIECE : (piece + 1) * PIECE]


def last_kernel(pre_v, pre_other, rhs, vb, *rest):
    ours, others, rest = rest[:PIECES], rest[PIECES : 2 * PIECES], rest[2 * PIECES :]
    labels, messages, rest = rest[0], rest[1:7], rest[7:]
    adjoint, residual, adjoint_v, residual_v, both, wide_a, wide_b, narrow_a, narrow_b, labels_s, label_sem, sems = rest
    core = lax.axis_index("blk")
    labels_copy = pltpu.make_async_copy(labels, labels_s, label_sem)
    labels_copy.start()
    wides, narrows = (wide_a, wide_b), (narrow_a, narrow_b)
    receive(labels_copy, labels_s, messages, ours, others, both, wides, narrows)

    def row(n, _):
        left = residual_of(n, rhs, both, wides, narrows)
        residual_v[n] = left
        fields = jnp.concatenate([rhs[n].astype(jnp.bfloat16), vb[n], left.astype(jnp.bfloat16)], axis=0)
        halves = [solve(fields, blocks[n]) for blocks in (pre_v, pre_other)]
        mine, theirs = [(half[0:ADJ] + half[ADJ : 2 * ADJ]) + half[2 * ADJ :] for half in halves]
        adjoint_v[n, :, 0:HALF] = jnp.where(core == 0, mine, theirs)
        adjoint_v[n, :, HALF:WIDTH] = jnp.where(core == 0, theirs, mine)
        return 0

    copies = []
    for piece in range(PARTS):
        rows = pl.ds(piece * (ROWS // PARTS), ROWS // PARTS)
        lax.fori_loop(piece * (ROWS // PARTS), (piece + 1) * (ROWS // PARTS), row, 0, unroll=True)
        for k, (a, b) in enumerate(((residual_v, residual), (adjoint_v, adjoint))):
            copies.append(pltpu.make_async_copy(a.at[rows], b.at[rows], sems.at[k, piece]))
            copies[-1].start()
    for copy in copies:
        copy.wait()


def call(kernel, name, out_shape, in_specs, out_specs, scratch_shapes, cost=None):
    params = pltpu.CompilerParams(vmem_limit_bytes=VMEM_LIMIT)
    return pl.pallas_call(kernel, out_shape=out_shape, in_specs=in_specs, out_specs=out_specs, scratch_shapes=scratch_shapes,
                          compiler_params=params, cost_estimate=cost, name=name)


def on_device(off_blocks, diag_blocks, precond, adj_rhs, col_owner, col_local):
    nrows = lax.axis_size("rows")
    offsets = (1, nrows - 1, 2, nrows - 2, nrows // 2, nrows // 2 + 1)
    shape, f32, bf16, i32 = jax.ShapeDtypeStruct, jnp.float32, jnp.bfloat16, jnp.int32
    field, half_blocks = shape((ROWS, ADJ, WIDTH), f32), shape((ROWS, HALF, WIDTH), bf16)
    pieces = [shape((PIECE, ADJ, WIDTH), f32)] * PIECES
    row_of_ints = shape((1, 128), i32)
    dma = pltpu.SemaphoreType.DMA

    def across(x):
        return lax.ppermute(x, "blk", [(0, 1), (1, 0)])

    def to_faces(x, p):
        pairs = [(2 * i + c, 2 * ((i + offsets[FACES[ORDER[p]][c][i % 4]]) % nrows) + c) for i in range(nrows) for c in range(2)]
        return lax.ppermute(x, ("rows", "blk"), pairs)

    def tie(*arrays):
        return lax.optimization_barrier(arrays)

    def exchange(mine, theirs, *later, chain=False):
        sums = []
        for m, t in zip(mine, theirs):
            if sums and chain:
                t, sums[0] = tie(t, sums[0])
            sums.append((m + across(t).astype(f32)).astype(bf16))
        got = [to_faces(x, p) for p, x in enumerate(sums)]
        later = lax.optimization_barrier((*sums, *later))[len(sums) :]
        return got, *later

    def hand_on(got, parts):
        for p in range(len(FACES)):
            if p == TIE:
                got[p], parts[0] = tie(got[p], parts[0])
            else:
                got[p] = tie(got[p], parts[0])[0]
        others = [across(x) for x in parts]
        forwarded = [across(g) if p != LAST else None for p, g in enumerate(got)]
        got[LAST], forwarded[0] = tie(got[LAST], forwarded[0])
        forwarded[LAST] = across(got[LAST])
        return parts, others, got, forwarded

    def in_hbm(*arrays):
        return [pltpu.with_memory_space_constraint(x, pltpu.HBM) for x in arrays]

    cost = pl.CostEstimate(flops=2 * ROWS * (FAN + 1) * ADJ * HALF * WIDTH, bytes_accessed=40_000_000, transcendentals=0)
    ints = [pltpu.SMEM((FAN, ROWS), i32)] * 2
    received = [pltpu.VMEM((ROWS, ADJ, WIDTH), f32)] + [pltpu.VMEM((ROWS + 1, ADJ, 128), f32)] * 4
    sums = pltpu.VMEM((ROWS + 1, ADJ, WIDTH), f32)
    owner, local = col_owner.T, col_local.T
    pre_other = across(precond)

    x_half, xb, pre_v, *messages = call(
        first_kernel,
        "first_remote_terms",
        [shape((ROWS, ADJ, HALF), f32), shape((ROWS, ADJ, HALF), bf16), half_blocks]
        + [shape((BODY + CAP, 128), f32)] * 3 + [shape((BODY + CAP, 128), bf16)] * 3,
        [HBM] * 5,
        [VM] * 9,
        [pltpu.VMEM((FAN * CAP, HALF, WIDTH), bf16), pltpu.VMEM((ROWS, ADJ, WIDTH), f32)] + ints
        + [pltpu.SMEM((1, 128), i32), dma((FAN * CAP,)), dma, dma((3,))],
    )(*in_hbm(off_blocks, precond, adj_rhs, owner, local))
    got, xb = exchange(messages[:3], messages[3:], xb)
    xb, pre_other = tie(xb, pre_other)
    off_v, diag_v, table, *partial = call(
        first_local_kernel,
        "first_local_terms",
        [shape((ROWS, FAN, HALF, WIDTH), bf16), half_blocks, row_of_ints] + pieces,
        [HBM, HBM, VM, HBM, HBM],
        [VM] * 2 + [SM] + [VM] * PIECES,
        [sums] + ints + [dma((2, CHUNKS)), dma((2,))],
        cost,
    )(*in_hbm(off_blocks, diag_blocks), xb, *in_hbm(owner, local))
    partial, other, got, forwarded = hand_on(got, list(partial))

    vb, xb, labels, *messages = call(
        middle_kernel,
        "middle_remote_terms",
        [shape((ROWS, ADJ, WIDTH), bf16), shape((ROWS, ADJ, HALF), bf16), row_of_ints]
        + [shape((BODY, 128), f32)] * 3 + [shape((BODY, 128), bf16)] * 3,
        [VM, VM, VM, ANY, VM] + [VM] * (2 * PIECES + 6),
        [VM] * 9,
        received + [pltpu.SMEM((1, 128), i32), pltpu.SMEM((1, 128), i32), dma((2,))],
    )(off_v, pre_v, adj_rhs, table, x_half, *partial, *other, *got, *forwarded)
    got, xb = exchange(messages[:3], messages[3:], xb, chain=False)
    partial = call(
        middle_local_kernel,
        "middle_local_terms",
        pieces,
        [VM, VM, VM, SM, SM],
        [VM] * PIECES,
        [sums],
        cost,
    )(off_v, diag_v, xb, owner, local)
    partial, other, got, forwarded = hand_on(got, list(partial))

    return call(
        last_kernel,
        "last_terms",
        [field, field],
        [VM] * (4 + 2 * PIECES) + [ANY] + [VM] * 6,
        [HBM] * 2,
        [pltpu.VMEM((ROWS, ADJ, WIDTH), f32)] * 2 + received + [pltpu.SMEM((1, 128), i32), dma, dma((2, PARTS))],
    )(pre_v, pre_other, adj_rhs, vb, *partial, *other, labels, *got, *forwarded)


def solution(mesh):
    in_specs = (
        P("rows", None, "blk", None),
        P("rows", "blk", None),
        P("rows", "blk", None),
        P("rows", None, None),
        P("rows", None),
        P("rows", None),
    )
    out_specs = (P("rows", None, None), P("rows", None, None))

    def program(*arrays):
        return tuple(on_device(*arrays))

    return jax.shard_map(program, mesh=mesh, in_specs=in_specs, out_specs=out_specs, check_vma=False)
```

```python
import jax
import jax.numpy as jnp
from jax import lax
from jax.experimental import pallas as pl
from jax.experimental.pallas import tpu as pltpu
from jax.sharding import PartitionSpec as P

ROWS = 32
FAN = 6
ADJ = 16
WIDTH = 192
HALF = 96
CAP = 16
WIDE = CAP * ADJ
BODY = WIDE + WIDE // 2
NEAR, SEAM, FAR = 0, 1, 2
ORDER = (FAR, SEAM, NEAR)
FACES = (
    ((0, 1, 0, 1), (2, 2, 3, 3)),
    ((1, 0, 1, 0), (3, 3, 2, 2)),
    ((5, 5, 5, 5), (4, 4, 4, 4)),
)
STRIDE = CAP + 1
COUNTS = FAN * STRIDE
CHUNKS = 8
PIECES = 2
TIE = 0
LAST = 2
PARTS = 4
UNROLL = 32
LOCAL_UNROLL = 16
PIECE = ROWS // PIECES
PER = ROWS // CHUNKS
VMEM_LIMIT = 24 * 1024 * 1024

VM = pl.BlockSpec(memory_space=pltpu.VMEM)
SM = pl.BlockSpec(memory_space=pltpu.SMEM)
ANY = pl.BlockSpec(memory_space=pl.ANY)
HBM = pl.BlockSpec(memory_space=pltpu.HBM)


def face_of(p, core, own):
    kind = lax.rem(own, 4)
    picks = []
    for faces in FACES[ORDER[p]]:
        pick = faces[3]
        for k in (2, 1, 0):
            pick = jnp.where(kind == k, faces[k], pick)
        picks.append(pick)
    return jnp.where(core == 0, *picks)


def solve(field, block):
    return lax.dot_general(field.astype(jnp.bfloat16), block, (((1,), (1,)), ((), ())), preferred_element_type=jnp.float32)


def faces_in_order(core, own):
    return [face_of(p, 1 - core if other else core, own) for p in range(len(FACES)) for other in (True, False)]


def remote_terms(core, own, table, x_of, block_of, mine, theirs, local=None):
    faces = faces_in_order(core, own)
    for p in range(len(FACES)):
        for other, out in ((True, theirs[p]), (False, mine[p])):
            face = faces[2 * p + (0 if other else 1)]
            count = table[0, COUNTS + face]
            for s in range(CAP // 2):
                terms = []
                for slot in (s, s + CAP // 2):
                    at = jnp.minimum(slot, count - 1)
                    entry = table[0, face * STRIDE + at]
                    terms.append(jnp.dot(x_of(entry), block_of(face, at, entry), preferred_element_type=jnp.float32))
                    out[slot * ADJ : (slot + 1) * ADJ] = terms[-1][:, 0:128].astype(out.dtype)
                    if local is not None and not other:
                        label = jnp.where(slot < count, local[face, entry] + 1, 0)
                        out[BODY + slot : BODY + slot + 1] = jnp.full((1, 128), label, jnp.int32).astype(jnp.float32)
                both = jnp.concatenate([terms[0][:, 128:WIDTH], terms[1][:, 128:WIDTH]], axis=1)
                out[WIDE + s * ADJ : WIDE + (s + 1) * ADJ] = both.astype(out.dtype)
            if local is not None and other:
                out[BODY:] = jnp.zeros((CAP, 128), out.dtype)


def list_face(face, own, owner, table):
    def entry(i, rank):
        table[0, face * STRIDE + rank] = i
        return rank + (owner[face, i] != own).astype(jnp.int32)

    table[0, COUNTS + face] = lax.fori_loop(0, ROWS, entry, jnp.int32(0), unroll=8)


def first_kernel(off, precond, rhs, owner, local, x_half, xb, pre_v, m0, m1, m2, t0, t1, t2,
                 blocks, rhs_v, owner_s, local_s, table, sems, pre_sem, small_sems):
    core, own = lax.axis_index("blk"), lax.axis_index("rows")
    copies = [pltpu.make_async_copy(a, b, small_sems.at[k]) for k, (a, b) in enumerate(((owner, owner_s), (local, local_s), (rhs, rhs_v)))]
    copies.append(pltpu.make_async_copy(precond, pre_v, pre_sem))
    for copy in copies:
        copy.start()
    copies[0].wait()

    def fetch(face, slot, entry):
        return pltpu.make_async_copy(off.at[entry, face], blocks.at[face * CAP + slot], sems.at[face * CAP + slot])

    def list_row(i, ranks):
        after = []
        for k in range(FAN):
            remote, rank = owner_s[k, i] != own, ranks[k]
            table[0, k * STRIDE + rank] = i

            @pl.when(remote)
            def _():
                fetch(k, rank, i).start()

            after.append(rank + remote.astype(jnp.int32))
        return tuple(after)

    counts = lax.fori_loop(0, ROWS, list_row, (jnp.int32(0),) * FAN, unroll=4)
    for k in range(FAN):
        table[0, COUNTS + k] = counts[k]
    for copy in copies[1:]:
        copy.wait()

    def row(n, _):
        x = solve(rhs_v[n], pre_v[n])
        x_half[n] = x
        xb[n] = x.astype(jnp.bfloat16)
        return 0

    lax.fori_loop(0, ROWS, row, 0, unroll=UNROLL)
    for k in range(FAN):
        for slot in range(CAP):

            @pl.when(slot < counts[k])
            def _():
                fetch(k, slot, 0).wait()

    remote_terms(core, own, table, lambda e: xb[e], lambda face, at, e: blocks[face * CAP + at], (m0, m1, m2), (t0, t1, t2), local_s)


def local_terms(first, last, own, xb, off_v, diag_v, owner, local, sums):
    def row(i, _):
        x = xb[i]
        places, terms = [i], [jnp.dot(x, diag_v[i], preferred_element_type=jnp.float32)]
        for k in range(FAN):
            places.append(jnp.where(owner[k, i] == own, local[k, i], ROWS))
            terms.append(jnp.dot(x, off_v[i, k], preferred_element_type=jnp.float32))
        for place, term in zip(places, terms):
            sums[place] = sums[place] + term
        return 0

    lax.fori_loop(first, last, row, 0, unroll=min(last - first, LOCAL_UNROLL))


def first_local_kernel(off, diag, xb, owner, local, off_v, diag_v, table, *rest):
    partial, (sums, owner_s, local_s, sems, small_sems) = rest[:PIECES], rest[PIECES:]
    own = lax.axis_index("rows")
    small = [pltpu.make_async_copy(a, b, small_sems.at[k]) for k, (a, b) in enumerate(((owner, owner_s), (local, local_s)))]
    for copy in small:
        copy.start()
    copies = []
    for chunk in range(CHUNKS):
        part = pl.ds(chunk * PER, PER)
        copies.append([pltpu.make_async_copy(a.at[part], b.at[part], sems.at[k, chunk]) for k, (a, b) in enumerate(((off, off_v), (diag, diag_v)))])
        for copy in copies[-1]:
            copy.start()
    sums[...] = jnp.zeros(sums.shape, sums.dtype)
    for copy in small:
        copy.wait()
    for face in range(FAN):
        list_face(face, own, owner_s, table)
    for chunk in range(CHUNKS):
        for copy in copies[chunk]:
            copy.wait()
        local_terms(chunk * PER, (chunk + 1) * PER, own, xb, off_v, diag_v, owner_s, local_s, sums)
    for piece in range(PIECES):
        partial[piece][...] = sums[piece * PIECE : (piece + 1) * PIECE]


def place(messages, label_of, first, narrow_sum, wide_sum):
    lane = lax.broadcasted_iota(jnp.int32, (ADJ, 128), 1)
    for p, message in enumerate(messages):
        for s in range(CAP // 2):
            at = []
            for slot in (s, s + CAP // 2):
                label = label_of(first + p * CAP + slot)
                at.append(jnp.where(label == 0, ROWS, label - 1))
                wide_sum[at[-1]] += message[slot * ADJ : (slot + 1) * ADJ].astype(jnp.float32)
            both = message[WIDE + s * ADJ : WIDE + (s + 1) * ADJ].astype(jnp.float32)
            narrow_sum[at[0]] += jnp.where(lane < 64, both, 0.0)
            narrow_sum[at[1]] += jnp.where(lane < 64, 0.0, both)


def gather_labels(messages, row):
    found = jnp.concatenate([m[BODY:].astype(jnp.float32) for m in messages], axis=0)
    rows = lax.broadcasted_iota(jnp.int32, found.shape, 0)
    lanes = lax.broadcasted_iota(jnp.int32, found.shape, 1)
    row[...] = jnp.sum(jnp.where(rows == lanes, found, 0.0), axis=0, keepdims=True).astype(jnp.int32)


def receive(labels_copy, labels_s, messages, ours, other, both, wides, narrows):
    for ref in (*wides, *narrows):
        ref[...] = jnp.zeros(ref.shape, ref.dtype)
    for piece in range(PIECES):
        both[piece * PIECE : (piece + 1) * PIECE] = ours[piece][...] + other[piece][...]
    labels_copy.wait()
    label_of = lambda at: labels_s[0, at]
    place(messages[:3], label_of, 0, narrows[0], wides[0])
    place(messages[3:], label_of, 3 * CAP, narrows[1], wides[1])


def residual_of(n, rhs, both, wides, narrows):
    narrow = narrows[0][n] + narrows[1][n]
    narrow = narrow + pltpu.roll(narrow, 64, 1)
    got = jnp.concatenate([wides[0][n] + wides[1][n], narrow[:, 0:64]], axis=1)
    return rhs[n] - (both[n] + got)


def middle_kernel(off_v, pre_v, rhs, table, x_before, *rest):
    ours, others, messages, rest = rest[:PIECES], rest[PIECES : 2 * PIECES], rest[2 * PIECES : 2 * PIECES + 6], rest[2 * PIECES + 6 :]
    vb, xb, labels, m0, m1, m2, t0, t1, t2, both, wide_a, wide_b, narrow_a, narrow_b, table_s, labels_s, sems = rest
    core, own = lax.axis_index("blk"), lax.axis_index("rows")
    table_copy = pltpu.make_async_copy(table, table_s, sems.at[0])
    table_copy.start()
    gather_labels(messages, labels)
    labels_copy = pltpu.make_async_copy(labels, labels_s, sems.at[1])
    labels_copy.start()
    wides, narrows = (wide_a, wide_b), (narrow_a, narrow_b)
    receive(labels_copy, labels_s, messages, ours, others, both, wides, narrows)

    def row(n, _):
        left = residual_of(n, rhs, both, wides, narrows).astype(jnp.bfloat16)
        vb[n] = left
        xb[n] = (x_before[n] + solve(left, pre_v[n])).astype(jnp.bfloat16)
        return 0

    lax.fori_loop(0, ROWS, row, 0, unroll=UNROLL)
    table_copy.wait()
    remote_terms(core, own, table_s, lambda e: xb[e], lambda face, at, e: off_v[e, face], (m0, m1, m2), (t0, t1, t2))


def middle_local_kernel(off_v, diag_v, xb, owner, local, *rest):
    partial, sums = rest[:PIECES], rest[PIECES]
    own = lax.axis_index("rows")
    sums[...] = jnp.zeros(sums.shape, sums.dtype)
    local_terms(0, ROWS, own, xb, off_v, diag_v, owner, local, sums)
    for piece in range(PIECES):
        partial[piece][...] = sums[piece * PIECE : (piece + 1) * PIECE]


def last_kernel(pre_v, pre_other, rhs, vb, *rest):
    ours, others, rest = rest[:PIECES], rest[PIECES : 2 * PIECES], rest[2 * PIECES :]
    labels, messages, rest = rest[0], rest[1:7], rest[7:]
    adjoint, residual, adjoint_v, residual_v, both, wide_a, wide_b, narrow_a, narrow_b, labels_s, label_sem, sems = rest
    core = lax.axis_index("blk")
    labels_copy = pltpu.make_async_copy(labels, labels_s, label_sem)
    labels_copy.start()
    wides, narrows = (wide_a, wide_b), (narrow_a, narrow_b)
    receive(labels_copy, labels_s, messages, ours, others, both, wides, narrows)

    def row(n, _):
        left = residual_of(n, rhs, both, wides, narrows)
        residual_v[n] = left
        fields = jnp.concatenate([rhs[n].astype(jnp.bfloat16), vb[n], left.astype(jnp.bfloat16)], axis=0)
        halves = [solve(fields, blocks[n]) for blocks in (pre_v, pre_other)]
        mine, theirs = [(half[0:ADJ] + half[ADJ : 2 * ADJ]) + half[2 * ADJ :] for half in halves]
        adjoint_v[n, :, 0:HALF] = jnp.where(core == 0, mine, theirs)
        adjoint_v[n, :, HALF:WIDTH] = jnp.where(core == 0, theirs, mine)
        return 0

    copies = []
    for piece in range(PARTS):
        rows = pl.ds(piece * (ROWS // PARTS), ROWS // PARTS)
        lax.fori_loop(piece * (ROWS // PARTS), (piece + 1) * (ROWS // PARTS), row, 0, unroll=True)
        for k, (a, b) in enumerate(((residual_v, residual), (adjoint_v, adjoint))):
            copies.append(pltpu.make_async_copy(a.at[rows], b.at[rows], sems.at[k, piece]))
            copies[-1].start()
    for copy in copies:
        copy.wait()


def call(kernel, name, out_shape, in_specs, out_specs, scratch_shapes, cost=None):
    params = pltpu.CompilerParams(vmem_limit_bytes=VMEM_LIMIT)
    return pl.pallas_call(kernel, out_shape=out_shape, in_specs=in_specs, out_specs=out_specs, scratch_shapes=scratch_shapes,
                          compiler_params=params, cost_estimate=cost, name=name)


def on_device(off_blocks, diag_blocks, precond, adj_rhs, col_owner, col_local):
    nrows = lax.axis_size("rows")
    offsets = (1, nrows - 1, 2, nrows - 2, nrows // 2, nrows // 2 + 1)
    shape, f32, bf16, i32 = jax.ShapeDtypeStruct, jnp.float32, jnp.bfloat16, jnp.int32
    field, half_blocks = shape((ROWS, ADJ, WIDTH), f32), shape((ROWS, HALF, WIDTH), bf16)
    pieces = [shape((PIECE, ADJ, WIDTH), f32)] * PIECES
    row_of_ints = shape((1, 128), i32)
    dma = pltpu.SemaphoreType.DMA

    def across(x):
        return lax.ppermute(x, "blk", [(0, 1), (1, 0)])

    def to_faces(x, p):
        pairs = [(2 * i + c, 2 * ((i + offsets[FACES[ORDER[p]][c][i % 4]]) % nrows) + c) for i in range(nrows) for c in range(2)]
        return lax.ppermute(x, ("rows", "blk"), pairs)

    def tie(*arrays):
        return lax.optimization_barrier(arrays)

    def exchange(mine, theirs, *later):
        sums = [(m + across(t).astype(f32)).astype(bf16) for m, t in zip(mine, theirs)]
        got = [to_faces(x, p) for p, x in enumerate(sums)]
        later = lax.optimization_barrier((*sums, *later))[len(sums) :]
        return got, *later

    def hand_on(got, parts):
        for p in range(len(FACES)):
            if p == TIE:
                got[p], parts[0] = tie(got[p], parts[0])
            else:
                got[p] = tie(got[p], parts[0])[0]
        others = [across(x) for x in parts]
        forwarded = [across(g) if p != LAST else None for p, g in enumerate(got)]
        got[LAST], forwarded[0] = tie(got[LAST], forwarded[0])
        forwarded[LAST] = across(got[LAST])
        return parts, others, got, forwarded

    def in_hbm(*arrays):
        return [pltpu.with_memory_space_constraint(x, pltpu.HBM) for x in arrays]

    cost = pl.CostEstimate(flops=2 * ROWS * (FAN + 1) * ADJ * HALF * WIDTH, bytes_accessed=40_000_000, transcendentals=0)
    ints = [pltpu.SMEM((FAN, ROWS), i32)] * 2
    received = [pltpu.VMEM((ROWS, ADJ, WIDTH), f32)] + [pltpu.VMEM((ROWS + 1, ADJ, 128), f32)] * 4
    sums = pltpu.VMEM((ROWS + 1, ADJ, WIDTH), f32)
    owner, local = col_owner.T, col_local.T
    pre_other = across(precond)

    x_half, xb, pre_v, *messages = call(
        first_kernel,
        "first_remote_terms",
        [shape((ROWS, ADJ, HALF), f32), shape((ROWS, ADJ, HALF), bf16), half_blocks]
        + [shape((BODY + CAP, 128), f32)] * 3 + [shape((BODY + CAP, 128), bf16)] * 3,
        [HBM] * 5,
        [VM] * 9,
        [pltpu.VMEM((FAN * CAP, HALF, WIDTH), bf16), pltpu.VMEM((ROWS, ADJ, WIDTH), f32)] + ints
        + [pltpu.SMEM((1, 128), i32), dma((FAN * CAP,)), dma, dma((3,))],
    )(*in_hbm(off_blocks, precond, adj_rhs, owner, local))
    got, xb = exchange(messages[:3], messages[3:], xb)
    xb, pre_other = tie(xb, pre_other)
    off_v, diag_v, table, *partial = call(
        first_local_kernel,
        "first_local_terms",
        [shape((ROWS, FAN, HALF, WIDTH), bf16), half_blocks, row_of_ints] + pieces,
        [HBM, HBM, VM, HBM, HBM],
        [VM] * 2 + [SM] + [VM] * PIECES,
        [sums] + ints + [dma((2, CHUNKS)), dma((2,))],
        cost,
    )(*in_hbm(off_blocks, diag_blocks), xb, *in_hbm(owner, local))
    partial, other, got, forwarded = hand_on(got, list(partial))

    vb, xb, labels, *messages = call(
        middle_kernel,
        "middle_remote_terms",
        [shape((ROWS, ADJ, WIDTH), bf16), shape((ROWS, ADJ, HALF), bf16), row_of_ints]
        + [shape((BODY, 128), f32)] * 3 + [shape((BODY, 128), bf16)] * 3,
        [VM, VM, VM, ANY, VM] + [VM] * (2 * PIECES + 6),
        [VM] * 9,
        received + [pltpu.SMEM((1, 128), i32), pltpu.SMEM((1, 128), i32), dma((2,))],
    )(off_v, pre_v, adj_rhs, table, x_half, *partial, *other, *got, *forwarded)
    got, xb = exchange(messages[:3], messages[3:], xb)
    partial = call(
        middle_local_kernel,
        "middle_local_terms",
        pieces,
        [VM, VM, VM, SM, SM],
        [VM] * PIECES,
        [sums],
        cost,
    )(off_v, diag_v, xb, owner, local)
    partial, other, got, forwarded = hand_on(got, list(partial))

    return call(
        last_kernel,
        "last_terms",
        [field, field],
        [VM] * (4 + 2 * PIECES) + [ANY] + [VM] * 6,
        [HBM] * 2,
        [pltpu.VMEM((ROWS, ADJ, WIDTH), f32)] * 2 + received + [pltpu.SMEM((1, 128), i32), dma, dma((2, PARTS))],
    )(pre_v, pre_other, adj_rhs, vb, *partial, *other, labels, *got, *forwarded)


def solution(mesh):
    in_specs = (
        P("rows", None, "blk", None),
        P("rows", "blk", None),
        P("rows", "blk", None),
        P("rows", None, None),
        P("rows", None),
        P("rows", None),
    )
    out_specs = (P("rows", None, None), P("rows", None, None))

    def program(*arrays):
        return tuple(on_device(*arrays))

    return jax.shard_map(program, mesh=mesh, in_specs=in_specs, out_specs=out_specs, check_vma=False)
```

```python
import jax
import jax.numpy as jnp
from jax import lax
from jax.experimental import pallas as pl
from jax.experimental.pallas import tpu as pltpu
from jax.sharding import PartitionSpec as P

ROWS = 32
FAN = 6
ADJ = 16
WIDTH = 192
HALF = 96
CAP = 16
WIDE = CAP * ADJ
BODY = WIDE + WIDE // 2
NEAR, SEAM, FAR = 0, 1, 2
ORDER = (FAR, SEAM, NEAR)
FACES = (
    ((0, 1, 0, 1), (2, 2, 3, 3)),
    ((1, 0, 1, 0), (3, 3, 2, 2)),
    ((5, 5, 5, 5), (4, 4, 4, 4)),
)
STRIDE = CAP + 1
COUNTS = FAN * STRIDE
CHUNKS = 8
PIECES = 2
TIE = 0
LAST = 2
PARTS = 4
UNROLL = 32
LOCAL_UNROLL = 16
PIECE = ROWS // PIECES
PER = ROWS // CHUNKS
VMEM_LIMIT = 24 * 1024 * 1024

VM = pl.BlockSpec(memory_space=pltpu.VMEM)
SM = pl.BlockSpec(memory_space=pltpu.SMEM)
ANY = pl.BlockSpec(memory_space=pl.ANY)
HBM = pl.BlockSpec(memory_space=pltpu.HBM)


def face_of(p, core, own):
    kind = lax.rem(own, 4)
    picks = []
    for faces in FACES[ORDER[p]]:
        pick = faces[3]
        for k in (2, 1, 0):
            pick = jnp.where(kind == k, faces[k], pick)
        picks.append(pick)
    return jnp.where(core == 0, *picks)


def solve(field, block):
    return lax.dot_general(field.astype(jnp.bfloat16), block, (((1,), (1,)), ((), ())), preferred_element_type=jnp.float32)


def faces_in_order(core, own):
    return [face_of(p, 1 - core if other else core, own) for p in range(len(FACES)) for other in (True, False)]


def remote_terms(core, own, table, x_of, block_of, mine, theirs, local=None):
    faces = faces_in_order(core, own)
    for p in range(len(FACES)):
        for other, out in ((True, theirs[p]), (False, mine[p])):
            face = faces[2 * p + (0 if other else 1)]
            count = table[0, COUNTS + face]
            for s in range(CAP // 2):
                terms = []
                for slot in (s, s + CAP // 2):
                    at = jnp.minimum(slot, count - 1)
                    entry = table[0, face * STRIDE + at]
                    terms.append(jnp.dot(x_of(entry), block_of(face, at, entry), preferred_element_type=jnp.float32))
                    out[slot * ADJ : (slot + 1) * ADJ] = terms[-1][:, 0:128].astype(out.dtype)
                    if local is not None and not other:
                        label = jnp.where(slot < count, local[face, entry] + 1, 0)
                        out[BODY + slot : BODY + slot + 1] = jnp.full((1, 128), label, jnp.int32).astype(jnp.float32)
                both = jnp.concatenate([terms[0][:, 128:WIDTH], terms[1][:, 128:WIDTH]], axis=1)
                out[WIDE + s * ADJ : WIDE + (s + 1) * ADJ] = both.astype(out.dtype)
            if local is not None and other:
                out[BODY:] = jnp.zeros((CAP, 128), out.dtype)


def list_face(face, own, owner, table):
    def entry(i, rank):
        table[0, face * STRIDE + rank] = i
        return rank + (owner[face, i] != own).astype(jnp.int32)

    table[0, COUNTS + face] = lax.fori_loop(0, ROWS, entry, jnp.int32(0), unroll=8)


def first_kernel(off, precond, rhs, owner, local, x_half, xb, pre_v, m0, m1, m2, t0, t1, t2,
                 blocks, rhs_v, owner_s, local_s, table, sems, pre_sem, small_sems):
    core, own = lax.axis_index("blk"), lax.axis_index("rows")
    copies = [pltpu.make_async_copy(a, b, small_sems.at[k]) for k, (a, b) in enumerate(((owner, owner_s), (local, local_s), (rhs, rhs_v)))]
    copies.append(pltpu.make_async_copy(precond, pre_v, pre_sem))
    for copy in copies:
        copy.start()
    copies[0].wait()

    def fetch(face, slot, entry):
        return pltpu.make_async_copy(off.at[entry, face], blocks.at[face * CAP + slot], sems.at[face * CAP + slot])

    def list_row(i, ranks):
        after = []
        for k in range(FAN):
            remote, rank = owner_s[k, i] != own, ranks[k]
            table[0, k * STRIDE + rank] = i

            @pl.when(remote)
            def _():
                fetch(k, rank, i).start()

            after.append(rank + remote.astype(jnp.int32))
        return tuple(after)

    counts = lax.fori_loop(0, ROWS, list_row, (jnp.int32(0),) * FAN, unroll=4)
    for k in range(FAN):
        table[0, COUNTS + k] = counts[k]
    for copy in copies[1:]:
        copy.wait()

    def row(n, _):
        x = solve(rhs_v[n], pre_v[n])
        x_half[n] = x
        xb[n] = x.astype(jnp.bfloat16)
        return 0

    lax.fori_loop(0, ROWS, row, 0, unroll=UNROLL)
    for k in range(FAN):
        for slot in range(CAP):

            @pl.when(slot < counts[k])
            def _():
                fetch(k, slot, 0).wait()

    remote_terms(core, own, table, lambda e: xb[e], lambda face, at, e: blocks[face * CAP + at], (m0, m1, m2), (t0, t1, t2), local_s)


def local_terms(first, last, own, xb, off_v, diag_v, owner, local, sums):
    def row(i, _):
        x = xb[i]
        places, terms = [i], [jnp.dot(x, diag_v[i], preferred_element_type=jnp.float32)]
        for k in range(FAN):
            places.append(jnp.where(owner[k, i] == own, local[k, i], ROWS))
            terms.append(jnp.dot(x, off_v[i, k], preferred_element_type=jnp.float32))
        for place, term in zip(places, terms):
            sums[place] = sums[place] + term
        return 0

    lax.fori_loop(first, last, row, 0, unroll=min(last - first, LOCAL_UNROLL))


def first_local_kernel(off, diag_v, xb, owner, local, off_v, table, *rest):
    partial, (sums, owner_s, local_s, sems, small_sems) = rest[:PIECES], rest[PIECES:]
    own = lax.axis_index("rows")
    small = [pltpu.make_async_copy(a, b, small_sems.at[k]) for k, (a, b) in enumerate(((owner, owner_s), (local, local_s)))]
    for copy in small:
        copy.start()
    copies = []
    for chunk in range(CHUNKS):
        part = pl.ds(chunk * PER, PER)
        copies.append([pltpu.make_async_copy(a.at[part], b.at[part], sems.at[k, chunk]) for k, (a, b) in enumerate(((off, off_v),))])
        for copy in copies[-1]:
            copy.start()
    sums[...] = jnp.zeros(sums.shape, sums.dtype)
    for copy in small:
        copy.wait()
    for face in range(FAN):
        list_face(face, own, owner_s, table)
    for chunk in range(CHUNKS):
        for copy in copies[chunk]:
            copy.wait()
        local_terms(chunk * PER, (chunk + 1) * PER, own, xb, off_v, diag_v, owner_s, local_s, sums)
    for piece in range(PIECES):
        partial[piece][...] = sums[piece * PIECE : (piece + 1) * PIECE]


def place(messages, label_of, first, narrow_sum, wide_sum):
    lane = lax.broadcasted_iota(jnp.int32, (ADJ, 128), 1)
    for p, message in enumerate(messages):
        for s in range(CAP // 2):
            at = []
            for slot in (s, s + CAP // 2):
                label = label_of(first + p * CAP + slot)
                at.append(jnp.where(label == 0, ROWS, label - 1))
                wide_sum[at[-1]] += message[slot * ADJ : (slot + 1) * ADJ].astype(jnp.float32)
            both = message[WIDE + s * ADJ : WIDE + (s + 1) * ADJ].astype(jnp.float32)
            narrow_sum[at[0]] += jnp.where(lane < 64, both, 0.0)
            narrow_sum[at[1]] += jnp.where(lane < 64, 0.0, both)


def gather_labels(messages, row):
    found = jnp.concatenate([m[BODY:].astype(jnp.float32) for m in messages], axis=0)
    rows = lax.broadcasted_iota(jnp.int32, found.shape, 0)
    lanes = lax.broadcasted_iota(jnp.int32, found.shape, 1)
    row[...] = jnp.sum(jnp.where(rows == lanes, found, 0.0), axis=0, keepdims=True).astype(jnp.int32)


def receive(labels_copy, labels_s, messages, ours, other, both, wides, narrows):
    for ref in (*wides, *narrows):
        ref[...] = jnp.zeros(ref.shape, ref.dtype)
    for piece in range(PIECES):
        both[piece * PIECE : (piece + 1) * PIECE] = ours[piece][...] + other[piece][...]
    labels_copy.wait()
    label_of = lambda at: labels_s[0, at]
    place(messages[:3], label_of, 0, narrows[0], wides[0])
    place(messages[3:], label_of, 3 * CAP, narrows[1], wides[1])


def residual_of(n, rhs, both, wides, narrows):
    narrow = narrows[0][n] + narrows[1][n]
    narrow = narrow + pltpu.roll(narrow, 64, 1)
    got = jnp.concatenate([wides[0][n] + wides[1][n], narrow[:, 0:64]], axis=1)
    return rhs[n] - (both[n] + got)


def middle_kernel(off_v, pre_v, rhs, table, x_before, *rest):
    ours, others, messages, rest = rest[:PIECES], rest[PIECES : 2 * PIECES], rest[2 * PIECES : 2 * PIECES + 6], rest[2 * PIECES + 6 :]
    vb, xb, labels, m0, m1, m2, t0, t1, t2, both, wide_a, wide_b, narrow_a, narrow_b, table_s, labels_s, sems = rest
    core, own = lax.axis_index("blk"), lax.axis_index("rows")
    table_copy = pltpu.make_async_copy(table, table_s, sems.at[0])
    table_copy.start()
    gather_labels(messages, labels)
    labels_copy = pltpu.make_async_copy(labels, labels_s, sems.at[1])
    labels_copy.start()
    wides, narrows = (wide_a, wide_b), (narrow_a, narrow_b)
    receive(labels_copy, labels_s, messages, ours, others, both, wides, narrows)

    def row(n, _):
        left = residual_of(n, rhs, both, wides, narrows).astype(jnp.bfloat16)
        vb[n] = left
        xb[n] = (x_before[n] + solve(left, pre_v[n])).astype(jnp.bfloat16)
        return 0

    lax.fori_loop(0, ROWS, row, 0, unroll=UNROLL)
    table_copy.wait()
    remote_terms(core, own, table_s, lambda e: xb[e], lambda face, at, e: off_v[e, face], (m0, m1, m2), (t0, t1, t2))


def middle_local_kernel(off_v, diag_v, xb, owner, local, *rest):
    partial, sums = rest[:PIECES], rest[PIECES]
    own = lax.axis_index("rows")
    sums[...] = jnp.zeros(sums.shape, sums.dtype)
    local_terms(0, ROWS, own, xb, off_v, diag_v, owner, local, sums)
    for piece in range(PIECES):
        partial[piece][...] = sums[piece * PIECE : (piece + 1) * PIECE]


def last_kernel(pre_v, pre_other, rhs, vb, *rest):
    ours, others, rest = rest[:PIECES], rest[PIECES : 2 * PIECES], rest[2 * PIECES :]
    labels, messages, rest = rest[0], rest[1:7], rest[7:]
    adjoint, residual, adjoint_v, residual_v, both, wide_a, wide_b, narrow_a, narrow_b, labels_s, label_sem, sems = rest
    core = lax.axis_index("blk")
    labels_copy = pltpu.make_async_copy(labels, labels_s, label_sem)
    labels_copy.start()
    wides, narrows = (wide_a, wide_b), (narrow_a, narrow_b)
    receive(labels_copy, labels_s, messages, ours, others, both, wides, narrows)

    def row(n, _):
        left = residual_of(n, rhs, both, wides, narrows)
        residual_v[n] = left
        fields = jnp.concatenate([rhs[n].astype(jnp.bfloat16), vb[n], left.astype(jnp.bfloat16)], axis=0)
        halves = [solve(fields, blocks[n]) for blocks in (pre_v, pre_other)]
        mine, theirs = [(half[0:ADJ] + half[ADJ : 2 * ADJ]) + half[2 * ADJ :] for half in halves]
        adjoint_v[n, :, 0:HALF] = jnp.where(core == 0, mine, theirs)
        adjoint_v[n, :, HALF:WIDTH] = jnp.where(core == 0, theirs, mine)
        return 0

    copies = []
    for piece in range(PARTS):
        rows = pl.ds(piece * (ROWS // PARTS), ROWS // PARTS)
        lax.fori_loop(piece * (ROWS // PARTS), (piece + 1) * (ROWS // PARTS), row, 0, unroll=True)
        for k, (a, b) in enumerate(((residual_v, residual), (adjoint_v, adjoint))):
            copies.append(pltpu.make_async_copy(a.at[rows], b.at[rows], sems.at[k, piece]))
            copies[-1].start()
    for copy in copies:
        copy.wait()


def call(kernel, name, out_shape, in_specs, out_specs, scratch_shapes, cost=None):
    params = pltpu.CompilerParams(vmem_limit_bytes=VMEM_LIMIT)
    return pl.pallas_call(kernel, out_shape=out_shape, in_specs=in_specs, out_specs=out_specs, scratch_shapes=scratch_shapes,
                          compiler_params=params, cost_estimate=cost, name=name)


def on_device(off_blocks, diag_blocks, precond, adj_rhs, col_owner, col_local):
    nrows = lax.axis_size("rows")
    offsets = (1, nrows - 1, 2, nrows - 2, nrows // 2, nrows // 2 + 1)
    shape, f32, bf16, i32 = jax.ShapeDtypeStruct, jnp.float32, jnp.bfloat16, jnp.int32
    field, half_blocks = shape((ROWS, ADJ, WIDTH), f32), shape((ROWS, HALF, WIDTH), bf16)
    pieces = [shape((PIECE, ADJ, WIDTH), f32)] * PIECES
    row_of_ints = shape((1, 128), i32)
    dma = pltpu.SemaphoreType.DMA

    def across(x):
        return lax.ppermute(x, "blk", [(0, 1), (1, 0)])

    def to_faces(x, p):
        pairs = [(2 * i + c, 2 * ((i + offsets[FACES[ORDER[p]][c][i % 4]]) % nrows) + c) for i in range(nrows) for c in range(2)]
        return lax.ppermute(x, ("rows", "blk"), pairs)

    def tie(*arrays):
        return lax.optimization_barrier(arrays)

    def exchange(mine, theirs, *later):
        sums = [(m + across(t).astype(f32)).astype(bf16) for m, t in zip(mine, theirs)]
        got = [to_faces(x, p) for p, x in enumerate(sums)]
        later = lax.optimization_barrier((*sums, *later))[len(sums) :]
        return got, *later

    def hand_on(got, parts):
        for p in range(len(FACES)):
            if p == TIE:
                got[p], parts[0] = tie(got[p], parts[0])
            else:
                got[p] = tie(got[p], parts[0])[0]
        others = [across(x) for x in parts]
        forwarded = [across(g) if p != LAST else None for p, g in enumerate(got)]
        got[LAST], forwarded[0] = tie(got[LAST], forwarded[0])
        forwarded[LAST] = across(got[LAST])
        return parts, others, got, forwarded

    def in_hbm(*arrays):
        return [pltpu.with_memory_space_constraint(x, pltpu.HBM) for x in arrays]

    cost = pl.CostEstimate(flops=2 * ROWS * (FAN + 1) * ADJ * HALF * WIDTH, bytes_accessed=40_000_000, transcendentals=0)
    ints = [pltpu.SMEM((FAN, ROWS), i32)] * 2
    received = [pltpu.VMEM((ROWS, ADJ, WIDTH), f32)] + [pltpu.VMEM((ROWS + 1, ADJ, 128), f32)] * 4
    sums = pltpu.VMEM((ROWS + 1, ADJ, WIDTH), f32)
    owner, local = col_owner.T, col_local.T
    pre_other = across(precond)

    x_half, xb, pre_v, *messages = call(
        first_kernel,
        "first_remote_terms",
        [shape((ROWS, ADJ, HALF), f32), shape((ROWS, ADJ, HALF), bf16), half_blocks]
        + [shape((BODY + CAP, 128), f32)] * 3 + [shape((BODY + CAP, 128), bf16)] * 3,
        [HBM] * 5,
        [VM] * 9,
        [pltpu.VMEM((FAN * CAP, HALF, WIDTH), bf16), pltpu.VMEM((ROWS, ADJ, WIDTH), f32)] + ints
        + [pltpu.SMEM((1, 128), i32), dma((FAN * CAP,)), dma, dma((3,))],
    )(*in_hbm(off_blocks, precond, adj_rhs, owner, local))
    got, xb = exchange(messages[:3], messages[3:], xb)
    xb, pre_other = tie(xb, pre_other)
    off_v, table, *partial = call(
        first_local_kernel,
        "first_local_terms",
        [shape((ROWS, FAN, HALF, WIDTH), bf16), row_of_ints] + pieces,
        [HBM, VM, VM, HBM, HBM],
        [VM, SM] + [VM] * PIECES,
        [sums] + ints + [dma((1, CHUNKS)), dma((2,))],
        cost,
    )(*in_hbm(off_blocks), diag_blocks, xb, *in_hbm(owner, local))
    partial, other, got, forwarded = hand_on(got, list(partial))

    vb, xb, labels, *messages = call(
        middle_kernel,
        "middle_remote_terms",
        [shape((ROWS, ADJ, WIDTH), bf16), shape((ROWS, ADJ, HALF), bf16), row_of_ints]
        + [shape((BODY, 128), f32)] * 3 + [shape((BODY, 128), bf16)] * 3,
        [VM, VM, VM, ANY, VM] + [VM] * (2 * PIECES + 6),
        [VM] * 9,
        received + [pltpu.SMEM((1, 128), i32), pltpu.SMEM((1, 128), i32), dma((2,))],
    )(off_v, pre_v, adj_rhs, table, x_half, *partial, *other, *got, *forwarded)
    got, xb = exchange(messages[:3], messages[3:], xb)
    partial = call(
        middle_local_kernel,
        "middle_local_terms",
        pieces,
        [VM, VM, VM, SM, SM],
        [VM] * PIECES,
        [sums],
        cost,
    )(off_v, diag_blocks, xb, owner, local)
    partial, other, got, forwarded = hand_on(got, list(partial))

    return call(
        last_kernel,
        "last_terms",
        [field, field],
        [VM] * (4 + 2 * PIECES) + [ANY] + [VM] * 6,
        [HBM] * 2,
        [pltpu.VMEM((ROWS, ADJ, WIDTH), f32)] * 2 + received + [pltpu.SMEM((1, 128), i32), dma, dma((2, PARTS))],
    )(pre_v, pre_other, adj_rhs, vb, *partial, *other, labels, *got, *forwarded)


def solution(mesh):
    in_specs = (
        P("rows", None, "blk", None),
        P("rows", "blk", None),
        P("rows", "blk", None),
        P("rows", None, None),
        P("rows", None),
        P("rows", None),
    )
    out_specs = (P("rows", None, None), P("rows", None, None))

    def program(*arrays):
        return tuple(on_device(*arrays))

    return jax.shard_map(program, mesh=mesh, in_specs=in_specs, out_specs=out_specs, check_vma=False)
```
